256 devices in a mesh: dp: 32 (over x, z), tensor: 8 (over y, core).
Axes of the slice: x: 4, y: 4, z: 8, core: 2. Of those that a mesh axis runs over, the one named last changes fastest.
Arguments:
- queries: bfloat16 [24576, 4096], P('dp', 'tensor'), may hold values from -6 to 6
- keys: bfloat16 [24576, 2048], P('dp', 'tensor'), may hold values from -6 to 6
- values: bfloat16 [24576, 2048], P('dp', 'tensor'), may hold values from -6 to 6
- out_grad: bfloat16 [24576, 4096], P('dp', 'tensor'), may hold values from -6 to 6
- query_weight: bfloat16 [4608, 4096], P(None, 'tensor'), may hold values from -0.09375 to 0.09375
- parents: int32 [192], P('dp'), may hold values from -1 to 186, as said below
- lengths: int32 [192], P('dp'), may hold values from 1 to 128
Outputs:
- key_grad: bfloat16 [24576, 2048], P('dp', 'tensor')
- value_grad: bfloat16 [24576, 2048], P('dp', 'tensor')
- hidden_grad: bfloat16 [4608, 24576], P('tensor', 'dp')
The draws below stay inside these ranges and needn't reach their ends.
Inputs may be any that keep to these rules, and one draw needn't show every extreme that they name: Node i is stored on dp index i div 6. Only the first node of each dp index can have children; every parent is such a node, a chain of parents has at most three links, and some node is a root.
All inputs are finite; a program needn't handle non-finite values.
Results may differ from the reference program's by a relative error of at most 0.02.
Values may be sent and summed in bfloat16 or wider, within the bound.
No kernel may reach another device: no remote copies, remote signals or barrier semaphores. Data moves between devices by JAX's collectives and lax.ppermute only.
A program may use at most 128 MiB of HBM per device.

```python
import jax
import jax.numpy as jnp
from jax import lax

WIDTH = 4608
HEADS = 32
KV_HEADS = 16
HEAD = 128
SOFTCAP = 50
BLOCK = 128
NB_DEV = 6
GROUP = 2
QSCALAR = 144
NODES = 192
TOKENS = 24576
N_TENSOR = 8


def draw_parents(key, part):
    key = jax.random.fold_in(key, 7)
    key_level, key_rank, key_weight, key_leaf = jax.random.split(key, 4)
    upper_count = NODES // NB_DEV
    upper_level = jax.random.randint(key_level, (upper_count,), 0, 3)
    upper_level = upper_level.at[0].set(0)
    scores = jax.random.randint(key_rank, (upper_count, upper_count), 0, 1 << 20) * upper_count + jnp.arange(upper_count)[None, :]
    allowed = upper_level[None, :] < upper_level[:, None]
    ranked = jnp.where(allowed, scores, -1)
    chosen = jnp.argmax(ranked, axis=1)
    upper_parent = jnp.where(jnp.any(allowed, axis=1), chosen * NB_DEV, -1)
    weight_table = jax.random.randint(key_weight, (upper_count,), 1, 9) ** 2
    bounds = jnp.cumsum(weight_table)
    leaf_draw = jax.random.randint(key_leaf, (NODES,), 0, bounds[-1])
    leaf_parent = jnp.searchsorted(bounds, leaf_draw, side='right') * NB_DEV
    node_ids = jnp.arange(NODES)
    leaf_parent = jnp.where(node_ids == NODES - 1, (upper_count - 1) * NB_DEV, leaf_parent)
    return jnp.where(node_ids % NB_DEV == 0, upper_parent[node_ids // NB_DEV], leaf_parent).astype(jnp.int32)


def shared_signs(key):
    return (jax.random.randint(key, (KV_HEADS, HEAD), 0, 2) * 2 - 1).astype(jnp.float32)


def drawn_part(key, rows):
    key_pick, key_strength, key_sign = jax.random.split(key, 3)
    picked = (jax.random.randint(key_pick, (rows, 1), 0, 12) == 0).astype(jnp.float32)
    strength = jax.random.uniform(key_strength, (rows, 1), jnp.float32, 1.0, 3.0)
    row_sign = (jax.random.randint(key_sign, (rows, 1), 0, 2) * 2 - 1).astype(jnp.float32)
    return picked * strength * row_sign


def draw_queries(key, part):
    signs = shared_signs(key)
    key = jax.random.fold_in(key, 11)
    key_noise, key_plant = jax.random.split(key, 2)
    direction = jnp.repeat(signs, GROUP, axis=0).reshape(1, HEADS * HEAD)
    shape = (TOKENS, HEADS * HEAD)
    noise = jax.random.truncated_normal(key_noise, -3.0, 3.0, shape, jnp.float32)
    return (noise + drawn_part(key_plant, TOKENS) * direction).astype(jnp.bfloat16)


def draw_keys(key, part):
    signs = shared_signs(key)
    key = jax.random.fold_in(key, 13)
    key_noise, key_plant = jax.random.split(key, 2)
    direction = signs.reshape(1, KV_HEADS * HEAD)
    shape = (TOKENS, KV_HEADS * HEAD)
    noise = jax.random.truncated_normal(key_noise, -3.0, 3.0, shape, jnp.float32)
    return (noise + drawn_part(key_plant, TOKENS) * direction).astype(jnp.bfloat16)


def plant(array, key, smallest, largest):
    index_at = [jax.random.randint(jax.random.fold_in(key, axis), (), 0, length) for axis, length in enumerate(array.shape)]
    widest = array.shape.index(max(array.shape))
    beside = index_at[:widest] + [(index_at[widest] + 1) % array.shape[widest]] + index_at[widest + 1:]
    return array.at[tuple(index_at)].set(smallest).at[tuple(beside)].set(largest)


def level_of(key, dims, shards, smallest, largest):
    gain = 1.0
    for position, parts in shards:
        steps = jax.random.uniform(jax.random.fold_in(jax.random.fold_in(key, 6), position), (parts,), jnp.float32, smallest / len(shards), largest / len(shards))
        gain = gain * jnp.repeat(jnp.exp(steps), dims[position] // parts).reshape((-1,) + (1,) * (len(dims) - 1 - position))
    return gain


def normal_values(key, extent, width, reach, shards=(), kind=jnp.bfloat16):
    entries = width * jax.random.normal(key, extent, jnp.float32)
    if shards:
        entries = entries * level_of(key, extent, shards, -0.22, 0.18)
    return jnp.clip(entries, -reach, reach).astype(kind)


def setup_inputs(seed: int = 0) -> dict:
    splits = jax.random.split(jax.random.key(seed), 8)
    return {
        "queries": draw_queries(jax.random.fold_in(splits[7], 71), 0),
        "keys": draw_keys(jax.random.fold_in(splits[7], 71), 0),
        "values": normal_values(splits[2], (TOKENS, KV_HEADS * HEAD), 1.0, 6.0, ((0, 32), (1, 8))),
        "out_grad": normal_values(splits[3], (TOKENS, HEADS * HEAD), 1.0, 6.0, ((0, 32), (1, 8))),
        "query_weight": normal_values(splits[4], (WIDTH, HEADS * HEAD), (HEADS * HEAD) ** -0.5, 0.09375, ((1, 8),)),
        "parents": draw_parents(jax.random.fold_in(splits[7], 71), 0),
        "lengths": plant(jax.random.randint(splits[6], (NODES,), 1, BLOCK + 1), jax.random.fold_in(splits[6], 1), 1, BLOCK).astype(jnp.int32),
    }


def node_grad(query_block, grad_block, key_block, value_block, key_lengths, query_length):
    scale = QSCALAR ** (-0.5)
    query_f = query_block.astype(jnp.float32)
    key_f = key_block.astype(jnp.float32)
    value_f = value_block.astype(jnp.float32)
    query_pos = jnp.arange(BLOCK)
    key_pos = jnp.arange(4 * BLOCK)
    key_part = key_pos // BLOCK
    key_inner = key_pos % BLOCK
    key_live = key_inner < key_lengths[key_part]
    causal = (key_part[None, :] > 0) | (key_inner[None, :] <= query_pos[:, None])
    key_mask = key_live[None, :] & causal
    raw = jnp.einsum('qhgd,khd->hgqk', query_f, key_f)
    squash = jnp.tanh(raw * scale / SOFTCAP)
    weights_exp = jnp.where(key_mask, jnp.exp(SOFTCAP * squash), 0.0)
    probs = weights_exp / lax.optimization_barrier(jnp.sum(weights_exp, axis=-1, keepdims=True))
    prob_half = probs.astype(jnp.bfloat16)
    query_live = query_pos < query_length
    live_grad = jnp.where(query_live[:, None, None, None], grad_block, jnp.zeros((), jnp.bfloat16))
    live_f = live_grad.astype(jnp.float32)
    grad_probs = jnp.einsum('qhgd,khd->hgqk', live_f, value_f)
    delta = lax.optimization_barrier(jnp.sum(probs * grad_probs, axis=-1, keepdims=True))
    grad_scores = (probs * (grad_probs - delta) * (1.0 - squash * squash) * scale).astype(jnp.bfloat16)
    score_f = grad_scores.astype(jnp.float32)
    query_grad = jnp.einsum('hgqk,khd->qhgd', score_f, key_f).astype(jnp.bfloat16)
    key_terms = jnp.einsum('hgqk,qhgd->khd', score_f, query_f)
    value_terms = jnp.einsum('hgqk,qhgd->khd', prob_half.astype(jnp.float32), live_f)
    return (query_grad, key_terms, value_terms)

def reference(queries, keys, values, out_grad, query_weight, parents, lengths):
    first_link = parents
    second_link = jnp.where(first_link >= 0, parents[jnp.maximum(first_link, 0)], -1)
    third_link = jnp.where(second_link >= 0, parents[jnp.maximum(second_link, 0)], -1)
    node_ids = jnp.arange(NODES, dtype=jnp.int32)
    block_ids = jnp.stack([node_ids, first_link, second_link, third_link], axis=1)
    block_valid = block_ids >= 0
    safe_ids = jnp.maximum(block_ids, 0).astype(jnp.int32)
    key_lengths = jnp.where(block_valid, lengths[safe_ids], 0)
    query_nodes = queries.reshape(NODES, BLOCK, KV_HEADS, GROUP, HEAD)
    grad_nodes = out_grad.reshape(NODES, BLOCK, KV_HEADS, GROUP, HEAD)
    key_nodes = keys.reshape(NODES, BLOCK, KV_HEADS, HEAD)
    value_nodes = values.reshape(NODES, BLOCK, KV_HEADS, HEAD)

    def visit(carry, node_id):
        key_total, value_total = carry
        chosen = safe_ids[node_id]
        key_sel = key_nodes[chosen].reshape(4 * BLOCK, KV_HEADS, HEAD)
        value_sel = value_nodes[chosen].reshape(4 * BLOCK, KV_HEADS, HEAD)
        query_grad, key_terms, value_terms = node_grad(query_nodes[node_id], grad_nodes[node_id], key_sel, value_sel, key_lengths[node_id], lengths[node_id])
        key_total = key_total.at[chosen].add(key_terms.reshape(4, BLOCK, KV_HEADS * HEAD))
        value_total = value_total.at[chosen].add(value_terms.reshape(4, BLOCK, KV_HEADS * HEAD))
        return ((key_total, value_total), query_grad)
    empty = jnp.zeros((NODES, BLOCK, KV_HEADS * HEAD), jnp.float32)
    (key_total, value_total), query_grads = lax.scan(visit, (empty, empty), node_ids)
    query_all = query_grads.reshape(TOKENS, HEADS * HEAD)
    columns = HEADS * HEAD // N_TENSOR

    def group_step(total, group_id):
        offset = (group_id * columns).astype(jnp.int32)
        weight_part = lax.dynamic_slice_in_dim(query_weight, offset, columns, 1)
        grad_part = lax.dynamic_slice_in_dim(query_all, offset, columns, 1)
        term = lax.dot_general(weight_part, grad_part, (((1,), (1,)), ((), ())), preferred_element_type=jnp.float32)
        return (total + term.astype(jnp.bfloat16).astype(jnp.float32), None)
    hidden_total, unused = lax.scan(group_step, jnp.zeros((WIDTH, TOKENS), jnp.float32), jnp.arange(N_TENSOR, dtype=jnp.int32))
    key_grad = key_total.reshape(TOKENS, KV_HEADS * HEAD).astype(jnp.bfloat16)
    value_grad = value_total.reshape(TOKENS, KV_HEADS * HEAD).astype(jnp.bfloat16)
    return (key_grad, value_grad, hidden_total.astype(jnp.bfloat16))
```

```python
import functools

import jax
import jax.numpy as jnp
from jax import lax
from jax.experimental import pallas as pl
from jax.experimental.pallas import tpu as pltpu
from jax.sharding import PartitionSpec as P

HEAD = 128
SOFTCAP = 50
BLOCK = 128
QSCALAR = 144
META = 16
NX = 4
F32, BF16 = jnp.float32, jnp.bfloat16


def dot(a, b, ca, cb):
    return lax.dot_general(a, b, (((ca,), (cb,)), ((), ())), preferred_element_type=F32)


def pack_kernel(node_count, info, k_ref, v_ref, a_ref, b_ref):
    a_ref[0:BLOCK] = k_ref[:, :HEAD]
    a_ref[BLOCK : 2 * BLOCK] = v_ref[:, :HEAD]
    b_ref[0:BLOCK] = k_ref[:, HEAD:]
    b_ref[BLOCK : 2 * BLOCK] = v_ref[:, HEAD:]
    parent = info[0]
    link = jnp.where(parent >= 0, lax.div(jnp.maximum(parent, 0), node_count), -1)
    lane = lax.broadcasted_iota(jnp.int32, (META, HEAD), 1)
    meta = jnp.where(lane == 0, link, info[node_count])
    a_ref[2 * BLOCK :] = meta.astype(F32).astype(BF16)


def attention_kernel(node_count, nz, info, q_ref, k_ref, v_ref, g_ref, *refs):
    parts_a, parts_b, refs = refs[: 2 * NX], refs[2 * NX : 2 * NX + nz], refs[2 * NX + nz :]
    kg_ref, vg_ref, qg_ref = refs[:3]
    outs_a, outs_b, refs = refs[3 : 3 + 2 * NX], refs[3 + 2 * NX : 3 + 2 * NX + nz], refs[3 + 2 * NX + nz :]
    far_a, far_b, acc_a, acc_b, meta_v, meta_s, sem, meta_sem = refs
    half = nz // 2
    node = pl.program_id(0)
    scale = QSCALAR ** (-0.5)

    @pl.when(node == 0)
    def _():
        copies = [
            pltpu.make_async_copy(
                parts_a[2 * sx + j], far_a.at[pl.ds(sx * nz + j * half, half)], sem.at[2 * sx + j]
            )
            for sx in range(NX)
            for j in range(2)
        ] + [
            pltpu.make_async_copy(parts_b[sz], far_b.at[pl.ds(sz * NX, NX)], sem.at[2 * NX + sz])
            for sz in range(nz)
        ]
        for copy in copies:
            copy.start()
        acc_a[...] = jnp.zeros_like(acc_a)
        acc_b[...] = jnp.zeros_like(acc_b)
        for copy in copies:
            copy.wait()
        meta = jnp.max(far_a[:, 2 * BLOCK :, :].astype(F32), axis=1)
        meta_v[...] = meta.astype(jnp.int32)
        copy = pltpu.make_async_copy(meta_v, meta_s, meta_sem)
        copy.start()
        copy.wait()

    x_me, z_me = info[2 * node_count], info[2 * node_count + 1]

    def place(link):
        safe = jnp.maximum(link, 0)
        lx = lax.div(safe, nz)
        sx = lax.rem(x_me - lx + NX, NX)
        sz = lax.rem(z_me - (safe - lx * nz) + nz, nz)
        return sx * nz + sz, sz * NX + sx

    parent = info[node]
    link = jnp.where(parent >= 0, lax.div(jnp.maximum(parent, 0), node_count), -1)
    slots, lens = [], [info[node_count + node]]
    for _ in range(3):
        slot_a, slot_b = place(link)
        slots.append((slot_a, slot_b))
        lens.append(jnp.where(link >= 0, meta_s[slot_a, 1], 0))
        link = jnp.where(link >= 0, meta_s[slot_a, 0], -1)

    cols = 2 * BLOCK
    key_row = lax.broadcasted_iota(jnp.int32, (BLOCK, cols), 0)
    query_col = lax.broadcasted_iota(jnp.int32, (BLOCK, cols), 1)
    query_col = jnp.where(query_col >= BLOCK, query_col - BLOCK, query_col)
    live = lax.broadcasted_iota(jnp.int32, (BLOCK, HEAD), 0) < lens[0]
    masks = [(key_row < lens[0]) & (key_row <= query_col)] + [key_row < m for m in lens[1:]]

    for h in range(2):
        far = (far_a, far_b)[h]
        acc = (acc_a, acc_b)[h]
        lo, mid, hi = 2 * h * HEAD, (2 * h + 1) * HEAD, (2 * h + 2) * HEAD
        q = jnp.concatenate([q_ref[:, lo:mid], q_ref[:, mid:hi]], axis=0)
        zero = jnp.zeros((), BF16)
        g = jnp.concatenate(
            [jnp.where(live, g_ref[:, lo:mid], zero), jnp.where(live, g_ref[:, mid:hi], zero)], axis=0
        )
        at = slice(h * HEAD, (h + 1) * HEAD)
        keys = [k_ref[:, at]] + [far[s[h], 0:BLOCK, :] for s in slots]
        vals = [v_ref[:, at]] + [far[s[h], BLOCK : 2 * BLOCK, :] for s in slots]
        squash, weight, grad = [], [], []
        total = jnp.zeros((1, cols), F32)
        mixed = jnp.zeros((1, cols), F32)
        for b in range(4):
            t = jnp.tanh(dot(keys[b], q, 1, 1) * (scale / SOFTCAP))
            e = jnp.where(masks[b], jnp.exp(SOFTCAP * t), 0.0)
            d = dot(vals[b], g, 1, 1)
            total += jnp.sum(e, axis=0, keepdims=True)
            mixed += jnp.sum(e * d, axis=0, keepdims=True)
            squash.append(t)
            weight.append(e)
            grad.append(d)
        inverse = 1.0 / total
        delta = mixed * inverse
        query_grad = jnp.zeros((HEAD, cols), F32)
        for b in range(4):
            p = weight[b] * inverse
            ds = (p * (grad[b] - delta) * (scale - scale * (squash[b] * squash[b]))).astype(BF16)
            dk = dot(ds, q, 1, 0)
            dv = dot(p.astype(BF16), g, 1, 0)
            query_grad += dot(keys[b], ds, 0, 0)
            if b == 0:
                kg_ref[:, at] = dk.astype(BF16)
                vg_ref[:, at] = dv.astype(BF16)

                @pl.when(node == 0)
                def _():
                    acc[0, 0:BLOCK, :] += dk
                    acc[0, BLOCK:, :] += dv
            else:
                slot = slots[b - 1][h]
                acc[slot, 0:BLOCK, :] += dk
                acc[slot, BLOCK:, :] += dv
        qg_ref[lo:mid] = query_grad[:, :BLOCK].astype(BF16)
        qg_ref[mid:hi] = query_grad[:, BLOCK:].astype(BF16)

    @pl.when(node == node_count - 1)
    def _():
        for sx in range(NX):
            for j in range(2):
                outs_a[2 * sx + j][...] = acc_a[sx * nz + j * half : sx * nz + (j + 1) * half].astype(BF16)
        for sz in range(nz):
            outs_b[sz][...] = acc_b[sz * NX : (sz + 1) * NX].astype(BF16)


def hidden_kernel(w_ref, qg_ref, out_ref):
    out_ref[...] = dot(w_ref[...], qg_ref[...], 1, 0).astype(BF16)


def local(queries, keys, values, out_grad, query_weight, parents, lengths, *, dp):
    node_count = parents.shape[0]
    rows, cols = queries.shape
    kv_cols = keys.shape[1]
    width = query_weight.shape[0]
    nz = dp // NX
    half = nz // 2

    def send(array, dx, dz):
        pairs = [
            (x * nz + z, ((x + dx) % NX) * nz + (z + dz) % nz) for x in range(NX) for z in range(nz)
        ]
        return lax.ppermute(array, "dp", pairs)

    def add(*terms):
        return sum(t.astype(F32) for t in terms).astype(BF16)

    me = lax.axis_index("dp")
    info = jnp.concatenate([parents, lengths, jnp.stack([me // nz, me % nz]).astype(jnp.int32)])
    smem = pl.BlockSpec(memory_space=pltpu.SMEM)
    pack_a, pack_b = pl.pallas_call(
        functools.partial(pack_kernel, node_count),
        grid=(1,),
        in_specs=[smem] + [pl.BlockSpec((BLOCK, kv_cols), lambda i: (0, 0))] * 2,
        out_specs=[
            pl.BlockSpec((2 * BLOCK + META, HEAD), lambda i: (0, 0)),
            pl.BlockSpec((2 * BLOCK, HEAD), lambda i: (0, 0)),
        ],
        out_shape=[
            jax.ShapeDtypeStruct((2 * BLOCK + META, HEAD), BF16),
            jax.ShapeDtypeStruct((2 * BLOCK, HEAD), BF16),
        ],
        name="pack",
    )(info, keys, values)

    line_a = [pack_a] + [send(pack_a, 0, s) for s in range(1, nz)]
    line_b = [pack_b] + [send(pack_b, s, 0) for s in range(1, NX)]
    near_a = [jnp.stack(line_a[:half]), jnp.stack(line_a[half:])]
    near_b = jnp.stack(line_b)
    after = [send(a, 1, 0) for a in near_a]
    before = [send(a, -1, 0) for a in near_a]
    opposite = [send(after[0], 1, 0), send(before[1], -1, 0)]
    parts_a = near_a + after + opposite + before
    parts_b = [near_b] + [None] * (nz - 1)
    for s in range(1, half + 1):
        parts_b[s] = send(parts_b[s - 1], 0, 1)
        if s < half:
            parts_b[nz - s] = send(parts_b[(nz - s + 1) % nz], 0, -1)

    any_spec = pl.BlockSpec(memory_space=pl.ANY)
    whole = lambda *shape: pl.BlockSpec(shape, lambda i: (0,) * len(shape))
    outs = pl.pallas_call(
        functools.partial(attention_kernel, node_count, nz),
        grid=(node_count,),
        in_specs=[
            smem,
            pl.BlockSpec((BLOCK, cols), lambda i: (i, 0)),
            pl.BlockSpec((BLOCK, kv_cols), lambda i: (i, 0)),
            pl.BlockSpec((BLOCK, kv_cols), lambda i: (i, 0)),
            pl.BlockSpec((BLOCK, cols), lambda i: (i, 0)),
        ]
        + [any_spec] * (2 * NX + nz),
        out_specs=[
            pl.BlockSpec((BLOCK, kv_cols), lambda i: (i, 0)),
            pl.BlockSpec((BLOCK, kv_cols), lambda i: (i, 0)),
            pl.BlockSpec((cols, BLOCK), lambda i: (0, i)),
        ]
        + [whole(half, 2 * BLOCK, HEAD)] * (2 * NX)
        + [whole(NX, 2 * BLOCK, HEAD)] * nz,
        out_shape=[
            jax.ShapeDtypeStruct((rows, kv_cols), BF16),
            jax.ShapeDtypeStruct((rows, kv_cols), BF16),
            jax.ShapeDtypeStruct((cols, rows), BF16),
        ]
        + [jax.ShapeDtypeStruct((half, 2 * BLOCK, HEAD), BF16)] * (2 * NX)
        + [jax.ShapeDtypeStruct((NX, 2 * BLOCK, HEAD), BF16)] * nz,
        scratch_shapes=[
            pltpu.VMEM((dp, 2 * BLOCK + META, HEAD), BF16),
            pltpu.VMEM((dp, 2 * BLOCK, HEAD), BF16),
            pltpu.VMEM((dp, 2 * BLOCK, HEAD), F32),
            pltpu.VMEM((dp, 2 * BLOCK, HEAD), F32),
            pltpu.VMEM((dp, HEAD), jnp.int32),
            pltpu.SMEM((dp, HEAD), jnp.int32),
            pltpu.SemaphoreType.DMA((2 * NX + nz,)),
            pltpu.SemaphoreType.DMA,
        ],
        compiler_params=pltpu.CompilerParams(vmem_limit_bytes=48 * 1024 * 1024),
        name="attention",
    )(info, queries, keys, values, out_grad, *parts_a, *parts_b)
    key_grad, value_grad, query_grad = outs[:3]
    terms_a, terms_b = outs[3 : 3 + 2 * NX], outs[3 + 2 * NX :]

    tensor = lax.axis_size("tensor")
    tile = width // 8
    hidden = pl.pallas_call(
        hidden_kernel,
        grid=(8,),
        in_specs=[
            pl.BlockSpec((tile, cols), lambda i: (i, 0)),
            pl.BlockSpec((cols, rows), lambda i: (0, 0)),
        ],
        out_specs=pl.BlockSpec((tile, rows), lambda i: (i, 0)),
        out_shape=jax.ShapeDtypeStruct((width, rows), BF16),
        compiler_params=pltpu.CompilerParams(vmem_limit_bytes=32 * 1024 * 1024),
        name="hidden",
    )(query_weight, query_grad)
    hidden_grad = lax.psum_scatter(hidden, "tensor", scatter_dimension=0, tiled=True)

    down = [None, None]
    up = [None, None]
    down[0] = send(add(terms_a[2], send(terms_a[4], -1, 0)), -1, 0)
    down[1] = send(terms_a[3], -1, 0)
    up[0] = send(terms_a[6], 1, 0)
    up[1] = send(add(terms_a[7], send(terms_a[5], 1, 0)), 1, 0)
    line_a = [
        add(terms_a[j][s], down[j][s], up[j][s]) for j in range(2) for s in range(half)
    ]
    sum_a = add(line_a[0], *[send(line_a[s], 0, -s) for s in range(1, nz)])
    low = send(terms_b[half], 0, -1)
    for s in range(half - 1, 0, -1):
        low = send(add(terms_b[s], low), 0, -1)
    high = send(terms_b[half + 1], 0, 1)
    for s in range(half + 2, nz):
        high = send(add(terms_b[s], high), 0, 1)
    line_b = [add(terms_b[0][s], low[s], high[s]) for s in range(NX)]
    sum_b = add(line_b[0], *[send(line_b[s], -s, 0) for s in range(1, NX)])
    first_key = jnp.concatenate([sum_a[:BLOCK], sum_b[:BLOCK]], axis=1)
    first_value = jnp.concatenate([sum_a[BLOCK:], sum_b[BLOCK:]], axis=1)
    key_grad = lax.dynamic_update_slice(key_grad, first_key, (0, 0))
    value_grad = lax.dynamic_update_slice(value_grad, first_value, (0, 0))
    return (key_grad, value_grad, hidden_grad)


def solution(mesh):
    in_specs = (
        P("dp", "tensor"),
        P("dp", "tensor"),
        P("dp", "tensor"),
        P("dp", "tensor"),
        P(None, "tensor"),
        P("dp"),
        P("dp"),
    )
    out_specs = (P("dp", "tensor"), P("dp", "tensor"), P("tensor", "dp"))
    return jax.shard_map(
        functools.partial(local, dp=mesh.shape["dp"]),
        mesh=mesh,
        in_specs=in_specs,
        out_specs=out_specs,
        check_vma=False,
    )
```

```python
import functools

import jax
import jax.numpy as jnp
from jax import lax
from jax.experimental import pallas as pl
from jax.experimental.pallas import tpu as pltpu
from jax.sharding import PartitionSpec as P

HEAD = 128
SOFTCAP = 50
BLOCK = 128
QSCALAR = 144
META = 16
NX = 4
F32, BF16 = jnp.float32, jnp.bfloat16


def dot(a, b, ca, cb):
    return lax.dot_general(a, b, (((ca,), (cb,)), ((), ())), preferred_element_type=F32)


def pack_kernel(node_count, parents, lengths, k_ref, v_ref, a_ref, b_ref):
    a_ref[0:BLOCK] = k_ref[:, :HEAD]
    a_ref[BLOCK : 2 * BLOCK] = v_ref[:, :HEAD]
    b_ref[0:BLOCK] = k_ref[:, HEAD:]
    b_ref[BLOCK : 2 * BLOCK] = v_ref[:, HEAD:]
    parent = parents[0]
    link = jnp.where(parent >= 0, lax.div(jnp.maximum(parent, 0), node_count), -1)
    lane = lax.broadcasted_iota(jnp.int32, (META, HEAD), 1)
    meta = jnp.where(lane == 0, link, lengths[0])
    a_ref[2 * BLOCK :] = meta.astype(F32).astype(BF16)


def main_kernel(node_count, nz, parents, lengths, spot, q_ref, k_ref, v_ref, g_ref, w_ref, *refs):
    parts, refs = refs[: 5 + nz], refs[5 + nz :]
    kg_ref, vg_ref, out_ref = refs[:3]
    terms, refs = refs[3 : 8 + nz], refs[8 + nz :]
    far_a, far_b, acc_a, acc_b, send_a, send_b, qg_ref, meta_v, meta_s, sem, out_sem, meta_sem = refs
    half = nz // 2
    step = pl.program_id(0)
    pieces = [(0, nz), (nz, nz), (3 * nz, nz), (2 * nz, half), (2 * nz + half, half)]
    ranges = [(0, at, size) for at, size in pieces] + [(1, sz * NX, NX) for sz in range(nz)]

    def copies_in():
        return [
            pltpu.make_async_copy(part, (far_a, far_b)[h].at[pl.ds(at, size)], sem.at[i])
            for i, (part, (h, at, size)) in enumerate(zip(parts, ranges))
        ]

    def copies_out():
        return [
            pltpu.make_async_copy((send_a, send_b)[h].at[pl.ds(at, size)], term, out_sem.at[i])
            for i, (term, (h, at, size)) in enumerate(zip(terms, ranges))
        ]

    @pl.when(step == 0)
    def _():
        for copy in copies_in():
            copy.start()
        acc_a[...] = jnp.zeros_like(acc_a)
        acc_b[...] = jnp.zeros_like(acc_b)
        for copy in copies_in():
            copy.wait()
        meta = jnp.max(far_a[:, 2 * BLOCK :, :].astype(F32), axis=1)
        meta_v[...] = meta.astype(jnp.int32)
        copy = pltpu.make_async_copy(meta_v, meta_s, meta_sem)
        copy.start()
        copy.wait()

    @pl.when(step < node_count)
    def _():
        attend(
            node_count, nz, step, parents, lengths, spot, meta_s, (far_a, far_b), (acc_a, acc_b),
            q_ref, k_ref, v_ref, g_ref, kg_ref, vg_ref, qg_ref,
        )

    @pl.when(step == node_count - 1)
    def _():
        send_a[...] = acc_a[...].astype(BF16)
        send_b[...] = acc_b[...].astype(BF16)
        for copy in copies_out():
            copy.start()

    @pl.when(step >= node_count)
    def _():
        out_ref[...] = dot(w_ref[...], qg_ref[...], 1, 0).astype(BF16)

    @pl.when(step == pl.num_programs(0) - 1)
    def _():
        for copy in copies_out():
            copy.wait()


def attend(
    node_count, nz, node, parents, lengths, spot, meta_s, far_refs, acc_refs,
    q_ref, k_ref, v_ref, g_ref, kg_ref, vg_ref, qg_ref,
):
    scale = QSCALAR ** (-0.5)
    x_me, z_me = spot[0], spot[1]
    here = pl.ds(pl.multiple_of(node * BLOCK, BLOCK), BLOCK)

    def place(link):
        safe = jnp.maximum(link, 0)
        lx = lax.div(safe, nz)
        sx = lax.rem(x_me - lx + NX, NX)
        sz = lax.rem(z_me - (safe - lx * nz) + nz, nz)
        return sx * nz + sz, sz * NX + sx

    parent = parents[node]
    link = jnp.where(parent >= 0, lax.div(jnp.maximum(parent, 0), node_count), -1)
    slots, lens = [], [lengths[node]]
    for _ in range(3):
        slot_a, slot_b = place(link)
        slots.append((slot_a, slot_b))
        lens.append(jnp.where(link >= 0, meta_s[slot_a, 1], 0))
        link = jnp.where(link >= 0, meta_s[slot_a, 0], -1)

    cols = 2 * BLOCK
    key_row = lax.broadcasted_iota(jnp.int32, (BLOCK, cols), 0)
    query_col = lax.broadcasted_iota(jnp.int32, (BLOCK, cols), 1)
    query_col = jnp.where(query_col >= BLOCK, query_col - BLOCK, query_col)
    live = lax.broadcasted_iota(jnp.int32, (BLOCK, HEAD), 0) < lens[0]
    masks = [(key_row < lens[0]) & (key_row <= query_col)] + [key_row < m for m in lens[1:]]

    for h in range(2):
        far = far_refs[h]
        acc = acc_refs[h]
        lo, mid, hi = 2 * h * HEAD, (2 * h + 1) * HEAD, (2 * h + 2) * HEAD
        q = jnp.concatenate([q_ref[:, lo:mid], q_ref[:, mid:hi]], axis=0)
        zero = jnp.zeros((), BF16)
        g = jnp.concatenate(
            [jnp.where(live, g_ref[:, lo:mid], zero), jnp.where(live, g_ref[:, mid:hi], zero)], axis=0
        )
        at = slice(h * HEAD, (h + 1) * HEAD)
        keys = [k_ref[:, at]] + [far[s[h], 0:BLOCK, :] for s in slots]
        vals = [v_ref[:, at]] + [far[s[h], BLOCK : 2 * BLOCK, :] for s in slots]
        squash, weight, grad = [], [], []
        total = jnp.zeros((1, cols), F32)
        mixed = jnp.zeros((1, cols), F32)
        for b in range(4):
            t = jnp.tanh(dot(keys[b], q, 1, 1) * (scale / SOFTCAP))
            e = jnp.where(masks[b], jnp.exp(SOFTCAP * t), 0.0)
            d = dot(vals[b], g, 1, 1)
            total += jnp.sum(e, axis=0, keepdims=True)
            mixed += jnp.sum(e * d, axis=0, keepdims=True)
            squash.append(t)
            weight.append(e)
            grad.append(d)
        inverse = 1.0 / total
        delta = mixed * inverse
        query_grad = jnp.zeros((HEAD, cols), F32)
        for b in range(4):
            p = weight[b] * inverse
            ds = (p * (grad[b] - delta) * (scale - scale * (squash[b] * squash[b]))).astype(BF16)
            dk = dot(ds, q, 1, 0)
            dv = dot(p.astype(BF16), g, 1, 0)
            query_grad += dot(keys[b], ds, 0, 0)
            if b == 0:
                kg_ref[:, at] = dk.astype(BF16)
                vg_ref[:, at] = dv.astype(BF16)

                @pl.when(node == 0)
                def _():
                    acc[0, 0:BLOCK, :] += dk
                    acc[0, BLOCK:, :] += dv
            else:
                slot = slots[b - 1][h]
                acc[slot, 0:BLOCK, :] += dk
                acc[slot, BLOCK:, :] += dv
        qg_ref[lo:mid, here] = query_grad[:, :BLOCK].astype(BF16)
        qg_ref[mid:hi, here] = query_grad[:, BLOCK:].astype(BF16)


def local(queries, keys, values, out_grad, query_weight, parents, lengths, *, dp):
    node_count = parents.shape[0]
    rows, cols = queries.shape
    kv_cols = keys.shape[1]
    width = query_weight.shape[0]
    nz = dp // NX
    half = nz // 2

    def send(array, dx, dz):
        pairs = [
            (x * nz + z, ((x + dx) % NX) * nz + (z + dz) % nz) for x in range(NX) for z in range(nz)
        ]
        return lax.ppermute(array, "dp", pairs)

    def add(*terms):
        return sum(t.astype(F32) for t in terms).astype(BF16)

    me = lax.axis_index("dp")
    spot = jnp.stack([me // nz, me % nz]).astype(jnp.int32)
    smem = pl.BlockSpec(memory_space=pltpu.SMEM)
    pack_a, pack_b = pl.pallas_call(
        functools.partial(pack_kernel, node_count),
        grid=(1,),
        in_specs=[smem, smem] + [pl.BlockSpec((BLOCK, kv_cols), lambda i: (0, 0))] * 2,
        out_specs=[
            pl.BlockSpec((2 * BLOCK + META, HEAD), lambda i: (0, 0)),
            pl.BlockSpec((2 * BLOCK, HEAD), lambda i: (0, 0)),
        ],
        out_shape=[
            jax.ShapeDtypeStruct((2 * BLOCK + META, HEAD), BF16),
            jax.ShapeDtypeStruct((2 * BLOCK, HEAD), BF16),
        ],
        name="pack",
    )(parents, lengths, keys, values)

    a1, a7, a2, a6 = (send(pack_a, 0, s) for s in (1, -1, 2, -2))
    b1, b3, b2 = (send(pack_b, s, 0) for s in (1, -1, 2))
    near_b = jnp.stack([pack_b, b1, b2, b3])
    a34 = send(jnp.stack([a1, a2]), 0, 2)
    a5 = send(a7, 0, -2)
    rings = [near_b] + [None] * (nz - 1)
    for s in range(1, half + 1):
        rings[s] = send(rings[s - 1], 0, 1)
        if s < half:
            rings[nz - s] = send(rings[(nz - s + 1) % nz], 0, -1)
    near_a = jnp.concatenate([jnp.stack([pack_a, a1, a2]), a34, jnp.stack([a5, a6, a7])])
    after, before = send(near_a, 1, 0), send(near_a, -1, 0)
    parts = [near_a, after, before, send(after[:half], 1, 0), send(before[half:], -1, 0)] + rings

    any_spec = pl.BlockSpec(memory_space=pl.ANY)
    tiles = 8
    tile = width // tiles
    node_map = lambda i: (jnp.minimum(i, node_count - 1), 0)
    tile_map = lambda i: (jnp.maximum(i - node_count, 0), 0)
    sizes = [nz, nz, nz, half, half] + [NX] * nz
    outs = pl.pallas_call(
        functools.partial(main_kernel, node_count, nz),
        grid=(node_count + tiles,),
        in_specs=[
            smem,
            smem,
            smem,
            pl.BlockSpec((BLOCK, cols), node_map),
            pl.BlockSpec((BLOCK, kv_cols), node_map),
            pl.BlockSpec((BLOCK, kv_cols), node_map),
            pl.BlockSpec((BLOCK, cols), node_map),
            pl.BlockSpec((tile, cols), tile_map),
        ]
        + [any_spec] * (5 + nz),
        out_specs=[
            pl.BlockSpec((BLOCK, kv_cols), node_map),
            pl.BlockSpec((BLOCK, kv_cols), node_map),
            pl.BlockSpec((tile, rows), tile_map),
        ]
        + [any_spec] * (5 + nz),
        out_shape=[
            jax.ShapeDtypeStruct((rows, kv_cols), BF16),
            jax.ShapeDtypeStruct((rows, kv_cols), BF16),
            jax.ShapeDtypeStruct((width, rows), BF16),
        ]
        + [jax.ShapeDtypeStruct((size, 2 * BLOCK, HEAD), BF16) for size in sizes],
        scratch_shapes=[
            pltpu.VMEM((dp, 2 * BLOCK + META, HEAD), BF16),
            pltpu.VMEM((dp, 2 * BLOCK, HEAD), BF16),
            pltpu.VMEM((dp, 2 * BLOCK, HEAD), F32),
            pltpu.VMEM((dp, 2 * BLOCK, HEAD), F32),
            pltpu.VMEM((dp, 2 * BLOCK, HEAD), BF16),
            pltpu.VMEM((dp, 2 * BLOCK, HEAD), BF16),
            pltpu.VMEM((cols, rows), BF16),
            pltpu.VMEM((dp, HEAD), jnp.int32),
            pltpu.SMEM((dp, HEAD), jnp.int32),
            pltpu.SemaphoreType.DMA((5 + nz,)),
            pltpu.SemaphoreType.DMA((5 + nz,)),
            pltpu.SemaphoreType.DMA,
        ],
        compiler_params=pltpu.CompilerParams(vmem_limit_bytes=58 * 1024 * 1024),
        name="attention",
    )(parents, lengths, spot, queries, keys, values, out_grad, query_weight, *parts)
    key_grad, value_grad, hidden = outs[:3]
    own, prev, succ, far_low, far_high = outs[3:8]
    terms = outs[8:]

    hidden_grad = lax.psum_scatter(hidden, "tensor", scatter_dimension=0, tiled=True)

    low_a, high_a = send(far_low, -1, 0), send(far_high, 1, 0)
    low, high = send(terms[half], 0, -1), send(terms[half + 1], 0, 1)
    low_a = send(jnp.concatenate([add(prev[:half], low_a), prev[half:]]), -1, 0)
    high_a = send(jnp.concatenate([succ[:half], add(succ[half:], high_a)]), 1, 0)
    for s in range(half - 1, 0, -1):
        low = send(add(terms[s], low), 0, -1)
    for s in range(half + 2, nz):
        high = send(add(terms[s], high), 0, 1)
    line = [add(own[s], low_a[s], high_a[s]) for s in range(nz)]
    s6 = send(line[6], 0, 2)
    s34 = send(jnp.stack(line[3:5]), 0, -2)
    s5 = send(line[5], 0, 2)
    s1 = send(add(line[1], s34[0]), 0, -1)
    s2 = send(add(line[2], s34[1]), 0, -2)
    s7 = send(add(line[7], s5), 0, 1)
    sum_a = add(line[0], s1, s2, s6, s7)
    line_b = [add(terms[0][s], low[s], high[s]) for s in range(NX)]
    sum_b = add(line_b[0], *[send(line_b[s], -s, 0) for s in range(1, NX)])
    first_key = jnp.concatenate([sum_a[:BLOCK], sum_b[:BLOCK]], axis=1)
    first_value = jnp.concatenate([sum_a[BLOCK:], sum_b[BLOCK:]], axis=1)
    key_grad = lax.dynamic_update_slice(key_grad, first_key, (0, 0))
    value_grad = lax.dynamic_update_slice(value_grad, first_value, (0, 0))
    return (key_grad, value_grad, hidden_grad)


def solution(mesh):
    in_specs = (
        P("dp", "tensor"),
        P("dp", "tensor"),
        P("dp", "tensor"),
        P("dp", "tensor"),
        P(None, "tensor"),
        P("dp"),
        P("dp"),
    )
    out_specs = (P("dp", "tensor"), P("dp", "tensor"), P("tensor", "dp"))
    return jax.shard_map(
        functools.partial(local, dp=mesh.shape["dp"]),
        mesh=mesh,
        in_specs=in_specs,
        out_specs=out_specs,
        check_vma=False,
    )
```

```python
import functools

import jax
import jax.numpy as jnp
from jax import lax
from jax.experimental import pallas as pl
from jax.experimental.pallas import tpu as pltpu
from jax.sharding import PartitionSpec as P

HEAD = 128
SOFTCAP = 50
BLOCK = 128
QSCALAR = 144
META = 16
TILES = 8
UNROLL = 3
NX = 4
F32, BF16 = jnp.float32, jnp.bfloat16


def dot(a, b, ca, cb):
    return lax.dot_general(a, b, (((ca,), (cb,)), ((), ())), preferred_element_type=F32)


def pack_kernel(node_count, parents, lengths, k_ref, v_ref, a_ref, b_ref):
    a_ref[0:BLOCK] = k_ref[:, :HEAD]
    a_ref[BLOCK : 2 * BLOCK] = v_ref[:, :HEAD]
    b_ref[0:BLOCK] = k_ref[:, HEAD:]
    b_ref[BLOCK : 2 * BLOCK] = v_ref[:, HEAD:]
    parent = parents[0]
    link = jnp.where(parent >= 0, lax.div(jnp.maximum(parent, 0), node_count), -1)
    lane = lax.broadcasted_iota(jnp.int32, (META, HEAD), 1)
    meta = jnp.where(lane == 0, link, lengths[0])
    a_ref[2 * BLOCK :] = meta.astype(F32).astype(BF16)


def head_kernel(h, node_count, nz, pieces, parents, lengths, spot, *refs):
    last = h == 1
    if last:
        table, refs = refs[0], refs[1:]
    q_hbm, k_hbm, v_hbm, g_hbm, *refs = refs
    if last:
        w_hbm, qg_in, kg_in, vg_in, *refs = refs
    parts, refs = refs[: len(pieces)], refs[len(pieces) :]
    kg_hbm, vg_hbm, *refs = refs
    if last:
        out_hbm, *refs = refs
    else:
        qg_out, table_out, *refs = refs
    terms, refs = refs[: len(pieces)], refs[len(pieces) :]
    q_ref, k_ref, v_ref, g_ref, kg_ref, vg_ref, qg_ref, far, acc, staged, *refs = refs
    if last:
        w_ref, out_ref, *refs = refs
    else:
        meta_v, table, *refs = refs
    sem, far_sem, term_sem, out_sem = refs
    copy = pltpu.make_async_copy
    lines = pl.ds(h * HEAD, HEAD)
    pair = pl.ds(2 * h * HEAD, 2 * HEAD)
    own_copies = [
        copy(q_hbm.at[:, pair], q_ref, sem.at[0]),
        copy(k_hbm.at[:, lines], k_ref, sem.at[1]),
        copy(v_hbm.at[:, lines], v_ref, sem.at[2]),
        copy(g_hbm.at[:, pair], g_ref, sem.at[3]),
    ]
    far_copies = [
        copy(part, far.at[pl.ds(at, size)], far_sem.at[i])
        for i, (part, (at, size)) in enumerate(zip(parts, pieces))
    ]
    term_copies = [
        copy(staged.at[pl.ds(at, size)], term, term_sem.at[i])
        for i, (term, (at, size)) in enumerate(zip(terms, pieces))
    ]
    grad_copies = [copy(kg_ref, kg_hbm, sem.at[4]), copy(vg_ref, vg_hbm, sem.at[5])]
    if last:
        late_copies = [
            copy(kg_in, kg_ref.at[:, pl.ds(0, HEAD)], sem.at[6]),
            copy(vg_in, vg_ref.at[:, pl.ds(0, HEAD)], sem.at[7]),
            copy(qg_in, qg_ref.at[pl.ds(0, 2 * HEAD)], sem.at[8]),
            copy(w_hbm, w_ref, sem.at[9]),
        ]
    else:
        late_copies = []
        table_copy = copy(meta_v, table, sem.at[6])
        grad_copies += [copy(qg_ref, qg_out, sem.at[7]), copy(meta_v, table_out, sem.at[8])]

    for c in far_copies + own_copies + late_copies:
        c.start()

    def clear(i, carry):
        acc[i] = jnp.zeros((2 * BLOCK, HEAD), F32)
        return carry

    lax.fori_loop(0, NX * nz + 1, clear, 0)
    for c in far_copies:
        c.wait()
    if not last:
        meta_v[...] = jnp.max(far[:, 2 * BLOCK :, :].astype(F32), axis=1).astype(jnp.int32)
        table_copy.start()
        table_copy.wait()
    for c in own_copies:
        c.wait()

    def node_step(node, carry):
        attend(
            h, node_count, nz, node, parents, lengths, spot, table, far, acc,
            q_ref, k_ref, v_ref, g_ref, kg_ref, vg_ref, qg_ref,
        )
        return carry

    lax.fori_loop(0, node_count, node_step, 0, unroll=UNROLL)

    def convert(i, carry):
        staged[i] = acc[i].astype(BF16)
        return carry

    lax.fori_loop(0, NX * nz, convert, 0)
    for c in term_copies:
        c.start()
    for c in late_copies:
        c.wait()
    for c in grad_copies:
        c.start()
    out_copies = []
    if last:
        tile = out_ref.shape[0] // TILES
        for i in range(TILES):
            at = slice(i * tile, (i + 1) * tile)
            out_ref[at, :] = dot(w_ref[at, :], qg_ref[...], 1, 0).astype(BF16)
            out_copies.append(copy(out_ref.at[at], out_hbm.at[at], out_sem.at[i]))
            out_copies[-1].start()
    for c in term_copies + grad_copies + out_copies:
        c.wait()


def attend(
    h, node_count, nz, node, parents, lengths, spot, table, far, acc,
    q_ref, k_ref, v_ref, g_ref, kg_ref, vg_ref, qg_ref,
):
    scale = QSCALAR ** (-0.5)
    x_me, z_me = spot[0], spot[1]
    here = pl.ds(pl.multiple_of(node * BLOCK, BLOCK), BLOCK)

    def place(link):
        safe = jnp.maximum(link, 0)
        lx = lax.div(safe, nz)
        sx = lax.rem(x_me - lx + NX, NX)
        sz = lax.rem(z_me - (safe - lx * nz) + nz, nz)
        return sx * nz + sz, sz * NX + sx

    parent = parents[node]
    link = jnp.where(parent >= 0, lax.div(jnp.maximum(parent, 0), node_count), -1)
    own_slot = jnp.where(node == 0, 0, NX * nz)
    slots, lens = [], [lengths[node]]
    for _ in range(3):
        both = place(link)
        slots.append(both[h])
        lens.append(jnp.where(link >= 0, table[both[0], 1], 0))
        link = jnp.where(link >= 0, table[both[0], 0], -1)

    cols = 2 * BLOCK
    key_row = lax.broadcasted_iota(jnp.int32, (BLOCK, cols), 0)
    query_col = lax.broadcasted_iota(jnp.int32, (BLOCK, cols), 1)
    query_col = jnp.where(query_col >= BLOCK, query_col - BLOCK, query_col)
    live = lax.broadcasted_iota(jnp.int32, (BLOCK, HEAD), 0) < lens[0]
    masks = [(key_row < lens[0]) & (key_row <= query_col)] + [key_row < m for m in lens[1:]]

    q = jnp.concatenate([q_ref[here, :HEAD], q_ref[here, HEAD:]], axis=0)
    zero = jnp.zeros((), BF16)
    g = jnp.concatenate(
        [jnp.where(live, g_ref[here, :HEAD], zero), jnp.where(live, g_ref[here, HEAD:], zero)], axis=0
    )
    at = slice(h * HEAD, (h + 1) * HEAD)
    keys = [k_ref[here, :]] + [far[s, 0:BLOCK, :] for s in slots]
    vals = [v_ref[here, :]] + [far[s, BLOCK : 2 * BLOCK, :] for s in slots]
    squash, weight, grad = [], [], []
    total = jnp.zeros((1, cols), F32)
    mixed = jnp.zeros((1, cols), F32)
    for b in range(4):
        t = jnp.tanh(dot(keys[b], q, 1, 1) * (scale / SOFTCAP))
        e = jnp.where(masks[b], jnp.exp(SOFTCAP * t), 0.0)
        d = dot(vals[b], g, 1, 1)
        total += jnp.sum(e, axis=0, keepdims=True)
        mixed += jnp.sum(e * d, axis=0, keepdims=True)
        squash.append(t)
        weight.append(e)
        grad.append(d)
    inverse = 1.0 / total
    delta = mixed * inverse
    query_grad = jnp.zeros((HEAD, cols), F32)
    for b in range(4):
        p = weight[b] * inverse
        ds = (p * (grad[b] - delta) * (scale - scale * (squash[b] * squash[b]))).astype(BF16)
        dk = dot(ds, q, 1, 0)
        dv = dot(p.astype(BF16), g, 1, 0)
        query_grad += dot(keys[b], ds, 0, 0)
        if b == 0:
            kg_ref[here, at] = dk.astype(BF16)
            vg_ref[here, at] = dv.astype(BF16)
        slot = slots[b - 1] if b else own_slot
        acc[slot, 0:BLOCK, :] += dk
        acc[slot, BLOCK:, :] += dv
    lo = 2 * h * HEAD
    qg_ref[lo : lo + HEAD, here] = query_grad[:, :BLOCK].astype(BF16)
    qg_ref[lo + HEAD : lo + 2 * HEAD, here] = query_grad[:, BLOCK:].astype(BF16)


def head_call(h, nz, pieces, scalars, arrays, extra, parts):
    last = h == 1
    queries, keys = arrays[:2]
    node_count = scalars[0].shape[0]
    rows, cols = queries.shape
    kv_cols = keys.shape[1]
    dp = NX * nz
    any_spec = pl.BlockSpec(memory_space=pl.ANY)
    smem = pl.BlockSpec(memory_space=pltpu.SMEM)
    wide = (h + 1) * HEAD
    far_rows = parts[0].shape[1]
    shape = jax.ShapeDtypeStruct
    out_shape = [shape((rows, wide), BF16)] * 2
    tail = []
    if last:
        width = extra[0].shape[0]
        out_shape += [shape((width, rows), BF16)]
        tail = [pltpu.VMEM((width, cols), BF16), pltpu.VMEM((width, rows), BF16)]
    else:
        out_shape += [shape((2 * wide, rows), BF16), shape((dp, HEAD), jnp.int32)]
        tail = [pltpu.VMEM((dp, HEAD), jnp.int32), pltpu.SMEM((dp, HEAD), jnp.int32)]
    out_shape += [shape((size, 2 * BLOCK, HEAD), BF16) for _, size in pieces]
    return pl.pallas_call(
        functools.partial(head_kernel, h, node_count, nz, pieces),
        in_specs=[smem] * len(scalars) + [any_spec] * (len(arrays) + len(extra) + len(parts)),
        out_specs=[any_spec] * len(out_shape),
        out_shape=out_shape,
        scratch_shapes=[
            pltpu.VMEM((rows, 2 * HEAD), BF16),
            pltpu.VMEM((rows, HEAD), BF16),
            pltpu.VMEM((rows, HEAD), BF16),
            pltpu.VMEM((rows, 2 * HEAD), BF16),
            pltpu.VMEM((rows, wide), BF16),
            pltpu.VMEM((rows, wide), BF16),
            pltpu.VMEM((2 * wide, rows), BF16),
            pltpu.VMEM((dp, far_rows, HEAD), BF16),
            pltpu.VMEM((dp + 1, 2 * BLOCK, HEAD), F32),
            pltpu.VMEM((dp, 2 * BLOCK, HEAD), BF16),
        ]
        + tail
        + [
            pltpu.SemaphoreType.DMA((10,)),
            pltpu.SemaphoreType.DMA((len(pieces),)),
            pltpu.SemaphoreType.DMA((len(pieces),)),
            pltpu.SemaphoreType.DMA((TILES,)),
        ],
        compiler_params=pltpu.CompilerParams(vmem_limit_bytes=58 * 1024 * 1024),
        name="second_head" if last else "first_head",
    )(*scalars, *arrays, *extra, *parts)


def main_calls(nz, parents, lengths, spot, queries, keys, values, out_grad, query_weight, parts):
    half = nz // 2
    arrays = (queries, keys, values, out_grad)
    pieces_a = [(0, nz), (nz, nz), (3 * nz, nz), (2 * nz, half), (2 * nz + half, half)]
    pieces_b = [(sz * NX, NX) for sz in range(nz)]
    kg, vg, qg, table, *terms_a = head_call(
        0, nz, pieces_a, (parents, lengths, spot), arrays, (), parts[:5]
    )
    key_grad, value_grad, hidden, *terms_b = head_call(
        1, nz, pieces_b, (parents, lengths, spot, table), arrays, (query_weight, qg, kg, vg), parts[5:]
    )
    return (key_grad, value_grad, hidden, *terms_a, *terms_b)


def local(queries, keys, values, out_grad, query_weight, parents, lengths, *, dp):
    node_count = parents.shape[0]
    kv_cols = keys.shape[1]
    nz = dp // NX
    half = nz // 2

    def send(array, dx, dz):
        pairs = [
            (x * nz + z, ((x + dx) % NX) * nz + (z + dz) % nz) for x in range(NX) for z in range(nz)
        ]
        return lax.ppermute(array, "dp", pairs)

    def add(*terms):
        return sum(t.astype(F32) for t in terms).astype(BF16)

    me = lax.axis_index("dp")
    spot = jnp.stack([me // nz, me % nz]).astype(jnp.int32)
    smem = pl.BlockSpec(memory_space=pltpu.SMEM)
    pack_a, pack_b = pl.pallas_call(
        functools.partial(pack_kernel, node_count),
        grid=(1,),
        in_specs=[smem, smem] + [pl.BlockSpec((BLOCK, kv_cols), lambda i: (0, 0))] * 2,
        out_specs=[
            pl.BlockSpec((2 * BLOCK + META, HEAD), lambda i: (0, 0)),
            pl.BlockSpec((2 * BLOCK, HEAD), lambda i: (0, 0)),
        ],
        out_shape=[
            jax.ShapeDtypeStruct((2 * BLOCK + META, HEAD), BF16),
            jax.ShapeDtypeStruct((2 * BLOCK, HEAD), BF16),
        ],
        name="pack",
    )(parents, lengths, keys, values)

    a1, a7, a2, a6 = (send(pack_a, 0, s) for s in (1, -1, 2, -2))
    b1, b3, b2 = (send(pack_b, s, 0) for s in (1, -1, 2))
    near_b = jnp.stack([pack_b, b1, b2, b3])
    a34 = send(jnp.stack([a1, a2]), 0, 2)
    a5 = send(a7, 0, -2)
    rings = [near_b] + [None] * (nz - 1)
    for s in range(1, half + 1):
        rings[s] = send(rings[s - 1], 0, 1)
        if s < half:
            rings[nz - s] = send(rings[(nz - s + 1) % nz], 0, -1)
    near_a = jnp.concatenate([jnp.stack([pack_a, a1, a2]), a34, jnp.stack([a5, a6, a7])])
    after, before = send(near_a, 1, 0), send(near_a, -1, 0)
    parts = [near_a, after, before, send(after[:half], 1, 0), send(before[half:], -1, 0)] + rings

    outs = main_calls(nz, parents, lengths, spot, queries, keys, values, out_grad, query_weight, parts)
    key_grad, value_grad, hidden = outs[:3]
    own, prev, succ, far_low, far_high = outs[3:8]
    terms = outs[8:]

    hidden_grad = lax.psum_scatter(hidden, "tensor", scatter_dimension=0, tiled=True)

    low_a, high_a = send(far_low, -1, 0), send(far_high, 1, 0)
    low, high = send(terms[half], 0, -1), send(terms[half + 1], 0, 1)
    low_a = send(jnp.concatenate([add(prev[:half], low_a), prev[half:]]), -1, 0)
    high_a = send(jnp.concatenate([succ[:half], add(succ[half:], high_a)]), 1, 0)
    for s in range(half - 1, 0, -1):
        low = send(add(terms[s], low), 0, -1)
    for s in range(half + 2, nz):
        high = send(add(terms[s], high), 0, 1)
    line = [add(own[s], low_a[s], high_a[s]) for s in range(nz)]
    s6 = send(line[6], 0, 2)
    s34 = send(jnp.stack(line[3:5]), 0, -2)
    s5 = send(line[5], 0, 2)
    s1 = send(add(line[1], s34[0]), 0, -1)
    s2 = send(add(line[2], s34[1]), 0, -2)
    s7 = send(add(line[7], s5), 0, 1)
    sum_a = add(line[0], s1, s2, s6, s7)
    line_b = [add(terms[0][s], low[s], high[s]) for s in range(NX)]
    sum_b = add(line_b[0], *[send(line_b[s], -s, 0) for s in range(1, NX)])
    first_key = jnp.concatenate([sum_a[:BLOCK], sum_b[:BLOCK]], axis=1)
    first_value = jnp.concatenate([sum_a[BLOCK:], sum_b[BLOCK:]], axis=1)
    key_grad = lax.dynamic_update_slice(key_grad, first_key, (0, 0))
    value_grad = lax.dynamic_update_slice(value_grad, first_value, (0, 0))
    return (key_grad, value_grad, hidden_grad)


def solution(mesh):
    in_specs = (
        P("dp", "tensor"),
        P("dp", "tensor"),
        P("dp", "tensor"),
        P("dp", "tensor"),
        P(None, "tensor"),
        P("dp"),
        P("dp"),
    )
    out_specs = (P("dp", "tensor"), P("dp", "tensor"), P("tensor", "dp"))
    return jax.shard_map(
        functools.partial(local, dp=mesh.shape["dp"]),
        mesh=mesh,
        in_specs=in_specs,
        out_specs=out_specs,
        check_vma=False,
    )
```

```python
import functools

import jax
import jax.numpy as jnp
from jax import lax
from jax.experimental import pallas as pl
from jax.experimental.pallas import tpu as pltpu
from jax.sharding import PartitionSpec as P

HEAD = 128
SOFTCAP = 50
BLOCK = 128
QSCALAR = 144
META = 16
TILES = 8
UNROLL = 3
NX = 4
F32, BF16 = jnp.float32, jnp.bfloat16


def dot(a, b, ca, cb):
    return lax.dot_general(a, b, (((ca,), (cb,)), ((), ())), preferred_element_type=F32)


def pack_kernel(node_count, parents, lengths, k_ref, v_ref, a_ref, b_ref):
    a_ref[0:BLOCK] = k_ref[:, :HEAD]
    a_ref[BLOCK : 2 * BLOCK] = v_ref[:, :HEAD]
    b_ref[0:BLOCK] = k_ref[:, HEAD:]
    b_ref[BLOCK : 2 * BLOCK] = v_ref[:, HEAD:]
    parent = parents[0]
    link = jnp.where(parent >= 0, lax.div(jnp.maximum(parent, 0), node_count), -1)
    lane = lax.broadcasted_iota(jnp.int32, (META, HEAD), 1)
    meta = jnp.where(lane == 0, link, lengths[0])
    a_ref[2 * BLOCK :] = meta.astype(F32).astype(BF16)


def head_kernel(h, node_count, nz, pieces, term_pieces, parents, lengths, spot, *refs):
    last = h == 1
    if last:
        table, refs = refs[0], refs[1:]
    q_hbm, k_hbm, v_hbm, g_hbm, *refs = refs
    if last:
        w_hbm, qg_in, kg_in, vg_in, *refs = refs
    parts, refs = refs[: len(pieces)], refs[len(pieces) :]
    kg_hbm, vg_hbm, *refs = refs
    if last:
        out_hbm, *refs = refs
    else:
        qg_out, table_out, *refs = refs
    terms, refs = refs[: len(term_pieces)], refs[len(term_pieces) :]
    q_ref, k_ref, v_ref, g_ref, kg_ref, vg_ref, qg_ref, far, acc, staged, *refs = refs
    if last:
        w_ref, out_ref, *refs = refs
    else:
        meta_v, table, *refs = refs
    sem, far_sem, term_sem, out_sem = refs
    copy = pltpu.make_async_copy
    lines = pl.ds(h * HEAD, HEAD)
    pair = pl.ds(2 * h * HEAD, 2 * HEAD)
    own_copies = [
        copy(q_hbm.at[:, pair], q_ref, sem.at[0]),
        copy(k_hbm.at[:, lines], k_ref, sem.at[1]),
        copy(v_hbm.at[:, lines], v_ref, sem.at[2]),
        copy(g_hbm.at[:, pair], g_ref, sem.at[3]),
    ]
    far_copies = [
        copy(part, far.at[pl.ds(at, size)], far_sem.at[i])
        for i, (part, (at, size)) in enumerate(zip(parts, pieces))
    ]
    term_copies = [
        copy(staged.at[pl.ds(at, size)], term, term_sem.at[i])
        for i, (term, (at, size)) in enumerate(zip(terms, term_pieces))
    ]
    grad_copies = [copy(kg_ref, kg_hbm, sem.at[4]), copy(vg_ref, vg_hbm, sem.at[5])]
    if last:
        late_copies = [
            copy(kg_in, kg_ref.at[:, pl.ds(0, HEAD)], sem.at[6]),
            copy(vg_in, vg_ref.at[:, pl.ds(0, HEAD)], sem.at[7]),
            copy(qg_in, qg_ref.at[pl.ds(0, 2 * HEAD)], sem.at[8]),
            copy(w_hbm, w_ref, sem.at[9]),
        ]
    else:
        late_copies = []
        table_copy = copy(meta_v, table, sem.at[6])
        grad_copies += [copy(qg_ref, qg_out, sem.at[7]), copy(meta_v, table_out, sem.at[8])]

    for c in far_copies + own_copies + late_copies:
        c.start()

    def clear(i, carry):
        acc[i] = jnp.zeros((2 * BLOCK, HEAD), F32)
        return carry

    lax.fori_loop(0, NX * nz + 1, clear, 0)
    for c in far_copies:
        c.wait()
    if not last:
        meta_v[...] = jnp.max(far[:, 2 * BLOCK :, :].astype(F32), axis=1).astype(jnp.int32)
        table_copy.start()
        table_copy.wait()
    for c in own_copies:
        c.wait()

    def node_step(node, carry):
        attend(
            h, node_count, nz, node, parents, lengths, spot, table, far, acc,
            q_ref, k_ref, v_ref, g_ref, kg_ref, vg_ref, qg_ref,
        )
        return carry

    lax.fori_loop(0, node_count, node_step, 0, unroll=UNROLL)

    def convert(i, carry):
        staged[i] = acc[i].astype(BF16)
        return carry

    lax.fori_loop(0, NX * nz, convert, 0)
    for c in term_copies:
        c.start()
    for c in late_copies:
        c.wait()
    for c in grad_copies:
        c.start()
    out_copies = []
    if last:
        tile = out_ref.shape[0] // TILES
        for i in range(TILES):
            at = slice(i * tile, (i + 1) * tile)
            out_ref[at, :] = dot(w_ref[at, :], qg_ref[...], 1, 0).astype(BF16)
            out_copies.append(copy(out_ref.at[at], out_hbm.at[at], out_sem.at[i]))
            out_copies[-1].start()
    for c in term_copies + grad_copies + out_copies:
        c.wait()


def attend(
    h, node_count, nz, node, parents, lengths, spot, table, far, acc,
    q_ref, k_ref, v_ref, g_ref, kg_ref, vg_ref, qg_ref,
):
    scale = QSCALAR ** (-0.5)
    x_me, z_me = spot[0], spot[1]
    here = pl.ds(pl.multiple_of(node * BLOCK, BLOCK), BLOCK)

    def place(link):
        safe = jnp.maximum(link, 0)
        lx = lax.div(safe, nz)
        sx = lax.rem(x_me - lx + NX, NX)
        sz = lax.rem(z_me - (safe - lx * nz) + nz, nz)
        return sx * nz + sz, sz * NX + sx, (safe - lx * nz) * NX + sx

    parent = parents[node]
    link = jnp.where(parent >= 0, lax.div(jnp.maximum(parent, 0), node_count), -1)
    own_slot = jnp.where(node == 0, 0, NX * nz)
    slots, sums, lens = [], [own_slot], [lengths[node]]
    for _ in range(3):
        both = place(link)
        slots.append(both[2 * h])
        sums.append(both[1 - h])
        lens.append(jnp.where(link >= 0, table[both[0], 1], 0))
        link = jnp.where(link >= 0, table[both[0], 0], -1)

    cols = 2 * BLOCK
    key_row = lax.broadcasted_iota(jnp.int32, (BLOCK, cols), 0)
    query_col = lax.broadcasted_iota(jnp.int32, (BLOCK, cols), 1)
    query_col = jnp.where(query_col >= BLOCK, query_col - BLOCK, query_col)
    live = lax.broadcasted_iota(jnp.int32, (BLOCK, HEAD), 0) < lens[0]
    masks = [(key_row < lens[0]) & (key_row <= query_col)] + [key_row < m for m in lens[1:]]

    q = jnp.concatenate([q_ref[here, :HEAD], q_ref[here, HEAD:]], axis=0)
    zero = jnp.zeros((), BF16)
    g = jnp.concatenate(
        [jnp.where(live, g_ref[here, :HEAD], zero), jnp.where(live, g_ref[here, HEAD:], zero)], axis=0
    )
    at = slice(h * HEAD, (h + 1) * HEAD)
    keys = [k_ref[here, :]] + [far[s, 0:BLOCK, :] for s in slots]
    vals = [v_ref[here, :]] + [far[s, BLOCK : 2 * BLOCK, :] for s in slots]
    squash, weight, grad = [], [], []
    total = jnp.zeros((1, cols), F32)
    mixed = jnp.zeros((1, cols), F32)
    for b in range(4):
        t = jnp.tanh(dot(keys[b], q, 1, 1) * (scale / SOFTCAP))
        e = jnp.where(masks[b], jnp.exp(SOFTCAP * t), 0.0)
        d = dot(vals[b], g, 1, 1)
        total += jnp.sum(e, axis=0, keepdims=True)
        mixed += jnp.sum(e * d, axis=0, keepdims=True)
        squash.append(t)
        weight.append(e)
        grad.append(d)
    inverse = 1.0 / total
    delta = mixed * inverse
    query_grad = jnp.zeros((HEAD, cols), F32)
    for b in range(4):
        p = weight[b] * inverse
        ds = (p * (grad[b] - delta) * (scale - scale * (squash[b] * squash[b]))).astype(BF16)
        dk = dot(ds, q, 1, 0)
        dv = dot(p.astype(BF16), g, 1, 0)
        query_grad += dot(keys[b], ds, 0, 0)
        if b == 0:
            kg_ref[here, at] = dk.astype(BF16)
            vg_ref[here, at] = dv.astype(BF16)
        acc[sums[b], 0:BLOCK, :] += dk
        acc[sums[b], BLOCK:, :] += dv
    lo = 2 * h * HEAD
    qg_ref[lo : lo + HEAD, here] = query_grad[:, :BLOCK].astype(BF16)
    qg_ref[lo + HEAD : lo + 2 * HEAD, here] = query_grad[:, BLOCK:].astype(BF16)


def head_call(h, nz, pieces, term_pieces, scalars, arrays, extra, parts):
    last = h == 1
    queries, keys = arrays[:2]
    node_count = scalars[0].shape[0]
    rows, cols = queries.shape
    kv_cols = keys.shape[1]
    dp = NX * nz
    any_spec = pl.BlockSpec(memory_space=pl.ANY)
    smem = pl.BlockSpec(memory_space=pltpu.SMEM)
    wide = (h + 1) * HEAD
    far_rows = parts[0].shape[1]
    shape = jax.ShapeDtypeStruct
    out_shape = [shape((rows, wide), BF16)] * 2
    tail = []
    if last:
        width = extra[0].shape[0]
        out_shape += [shape((width, rows), BF16)]
        tail = [pltpu.VMEM((width, cols), BF16), pltpu.VMEM((width, rows), BF16)]
    else:
        out_shape += [shape((2 * wide, rows), BF16), shape((dp, HEAD), jnp.int32)]
        tail = [pltpu.VMEM((dp, HEAD), jnp.int32), pltpu.SMEM((dp, HEAD), jnp.int32)]
    out_shape += [shape((size, 2 * BLOCK, HEAD), BF16) for _, size in term_pieces]
    return pl.pallas_call(
        functools.partial(head_kernel, h, node_count, nz, pieces, term_pieces),
        in_specs=[smem] * len(scalars) + [any_spec] * (len(arrays) + len(extra) + len(parts)),
        out_specs=[any_spec] * len(out_shape),
        out_shape=out_shape,
        scratch_shapes=[
            pltpu.VMEM((rows, 2 * HEAD), BF16),
            pltpu.VMEM((rows, HEAD), BF16),
            pltpu.VMEM((rows, HEAD), BF16),
            pltpu.VMEM((rows, 2 * HEAD), BF16),
            pltpu.VMEM((rows, wide), BF16),
            pltpu.VMEM((rows, wide), BF16),
            pltpu.VMEM((2 * wide, rows), BF16),
            pltpu.VMEM((dp, far_rows, HEAD), BF16),
            pltpu.VMEM((dp + 1, 2 * BLOCK, HEAD), F32),
            pltpu.VMEM((dp, 2 * BLOCK, HEAD), BF16),
        ]
        + tail
        + [
            pltpu.SemaphoreType.DMA((10,)),
            pltpu.SemaphoreType.DMA((len(pieces),)),
            pltpu.SemaphoreType.DMA((len(term_pieces),)),
            pltpu.SemaphoreType.DMA((TILES,)),
        ],
        compiler_params=pltpu.CompilerParams(vmem_limit_bytes=58 * 1024 * 1024),
        name="second_head" if last else "first_head",
    )(*scalars, *arrays, *extra, *parts)


def local(queries, keys, values, out_grad, query_weight, parents, lengths, *, dp):
    node_count = parents.shape[0]
    kv_cols = keys.shape[1]
    nz = dp // NX
    half = nz // 2

    def send(array, dx, dz):
        pairs = [
            (x * nz + z, ((x + dx) % NX) * nz + (z + dz) % nz) for x in range(NX) for z in range(nz)
        ]
        return lax.ppermute(array, "dp", pairs)

    def add(*terms):
        return sum(t.astype(F32) for t in terms).astype(BF16)

    me = lax.axis_index("dp")
    spot = jnp.stack([me // nz, me % nz]).astype(jnp.int32)
    smem = pl.BlockSpec(memory_space=pltpu.SMEM)
    pack_a, pack_b = pl.pallas_call(
        functools.partial(pack_kernel, node_count),
        grid=(1,),
        in_specs=[smem, smem] + [pl.BlockSpec((BLOCK, kv_cols), lambda i: (0, 0))] * 2,
        out_specs=[
            pl.BlockSpec((2 * BLOCK + META, HEAD), lambda i: (0, 0)),
            pl.BlockSpec((2 * BLOCK, HEAD), lambda i: (0, 0)),
        ],
        out_shape=[
            jax.ShapeDtypeStruct((2 * BLOCK + META, HEAD), BF16),
            jax.ShapeDtypeStruct((2 * BLOCK, HEAD), BF16),
        ],
        name="pack",
    )(parents, lengths, keys, values)

    b1, b3, b2 = (send(pack_b, s, 0) for s in (1, -1, 2))
    near_b = jnp.stack([pack_b, b1, b2, b3])
    columns = [[x * nz + z for z in range(nz)] for x in range(NX)]
    gathered = lax.all_gather(near_b, "dp", axis_index_groups=columns, axis=0, tiled=True)
    a1, a7, a2, a6 = (send(pack_a, 0, s) for s in (1, -1, 2, -2))
    a34 = send(jnp.stack([a1, a2]), 0, 2)
    a5 = send(a7, 0, -2)
    near_a = jnp.concatenate([jnp.stack([pack_a, a1, a2]), a34, jnp.stack([a5, a6, a7])])
    after, before = send(near_a, 1, 0), send(near_a, -1, 0)
    parts = [near_a, after, before, send(after[:half], 1, 0), send(before[half:], -1, 0)]

    arrays = (queries, keys, values, out_grad)
    five = [(0, nz), (nz, nz), (3 * nz, nz), (2 * nz, half), (2 * nz + half, half)]
    many = [(sz * NX, NX) for sz in range(nz)]
    scalars = (parents, lengths, spot)
    kg, vg, qg, table, *terms = head_call(0, nz, five, many, scalars, arrays, (), parts)
    low, high = send(terms[half], 0, -1), send(terms[half + 1], 0, 1)
    low, high = add(terms[half - 1], low), add(terms[half + 2], high)
    gathered, low, high = lax.optimization_barrier((gathered, low, high))
    low, high = send(low, 0, -1), send(high, 0, 1)
    key_grad, value_grad, hidden, *more = head_call(
        1, nz, [(0, dp)], five, (*scalars, table), arrays, (query_weight, qg, kg, vg), [gathered]
    )
    own, prev, succ, far_low, far_high = more

    hidden_grad = lax.psum_scatter(hidden, "tensor", scatter_dimension=0, tiled=True)

    low_a, high_a = send(far_low, -1, 0), send(far_high, 1, 0)
    low_a = send(jnp.concatenate([add(prev[:half], low_a), prev[half:]]), -1, 0)
    high_a = send(jnp.concatenate([succ[:half], add(succ[half:], high_a)]), 1, 0)
    for s in range(half - 2, 0, -1):
        low = send(add(terms[s], low), 0, -1)
    for s in range(half + 3, nz):
        high = send(add(terms[s], high), 0, 1)
    line = [add(own[s], low_a[s], high_a[s]) for s in range(nz)]
    s6 = send(line[6], 0, 2)
    s34 = send(jnp.stack(line[3:5]), 0, -2)
    s5 = send(line[5], 0, 2)
    s1 = send(add(line[1], s34[0]), 0, -1)
    s2 = send(add(line[2], s34[1]), 0, -2)
    s7 = send(add(line[7], s5), 0, 1)
    sum_a = add(line[0], s1, s2, s6, s7)
    line_b = [add(terms[0][s], low[s], high[s]) for s in range(NX)]
    sum_b = add(line_b[0], *[send(line_b[s], -s, 0) for s in range(1, NX)])
    first_key = jnp.concatenate([sum_b[:BLOCK], sum_a[:BLOCK]], axis=1)
    first_value = jnp.concatenate([sum_b[BLOCK:], sum_a[BLOCK:]], axis=1)
    key_grad = lax.dynamic_update_slice(key_grad, first_key, (0, 0))
    value_grad = lax.dynamic_update_slice(value_grad, first_value, (0, 0))
    return (key_grad, value_grad, hidden_grad)


def solution(mesh):
    in_specs = (
        P("dp", "tensor"),
        P("dp", "tensor"),
        P("dp", "tensor"),
        P("dp", "tensor"),
        P(None, "tensor"),
        P("dp"),
        P("dp"),
    )
    out_specs = (P("dp", "tensor"), P("dp", "tensor"), P("tensor", "dp"))
    return jax.shard_map(
        functools.partial(local, dp=mesh.shape["dp"]),
        mesh=mesh,
        in_specs=in_specs,
        out_specs=out_specs,
        check_vma=False,
    )
```

```python
import functools

import jax
import jax.numpy as jnp
from jax import lax
from jax.experimental import pallas as pl
from jax.experimental.pallas import tpu as pltpu
from jax.sharding import PartitionSpec as P

HEAD = 128
SOFTCAP = 50
BLOCK = 128
QSCALAR = 144
META = 16
TILES = 8
UNROLL = 3
NX = 4
F32, BF16 = jnp.float32, jnp.bfloat16


def dot(a, b, ca, cb):
    return lax.dot_general(a, b, (((ca,), (cb,)), ((), ())), preferred_element_type=F32)


def pack_kernel(node_count, parents, lengths, k_ref, v_ref, a_ref, b_ref):
    a_ref[0:BLOCK] = k_ref[:, :HEAD]
    a_ref[BLOCK : 2 * BLOCK] = v_ref[:, :HEAD]
    b_ref[0:BLOCK] = k_ref[:, HEAD:]
    b_ref[BLOCK : 2 * BLOCK] = v_ref[:, HEAD:]
    parent = parents[0]
    link = jnp.where(parent >= 0, lax.div(jnp.maximum(parent, 0), node_count), -1)
    lane = lax.broadcasted_iota(jnp.int32, (META, HEAD), 1)
    meta = jnp.where(lane == 0, link, lengths[0])
    a_ref[2 * BLOCK :] = meta.astype(F32).astype(BF16)


def head_kernel(h, node_count, nz, pieces, term_pieces, parents, lengths, spot, *refs):
    last = h == 1
    if last:
        table, refs = refs[0], refs[1:]
    q_hbm, k_hbm, v_hbm, g_hbm, *refs = refs
    if last:
        w_hbm, qg_in, kg_in, vg_in, *refs = refs
    parts, refs = refs[: len(pieces)], refs[len(pieces) :]
    kg_hbm, vg_hbm, *refs = refs
    if last:
        out_hbm, *refs = refs
    else:
        qg_out, table_out, *refs = refs
    terms, refs = refs[: len(term_pieces)], refs[len(term_pieces) :]
    q_ref, k_ref, v_ref, g_ref, kg_ref, vg_ref, qg_ref, far, acc, staged, *refs = refs
    if last:
        w_ref, out_ref, *refs = refs
    else:
        meta_v, table, *refs = refs
    sem, far_sem, term_sem, out_sem = refs
    copy = pltpu.make_async_copy
    lines = pl.ds(h * HEAD, HEAD)
    pair = pl.ds(2 * h * HEAD, 2 * HEAD)
    own_copies = [
        copy(q_hbm.at[:, pair], q_ref, sem.at[0]),
        copy(k_hbm.at[:, lines], k_ref, sem.at[1]),
        copy(v_hbm.at[:, lines], v_ref, sem.at[2]),
        copy(g_hbm.at[:, pair], g_ref, sem.at[3]),
    ]
    far_copies = [
        copy(part, far.at[pl.ds(at, size)], far_sem.at[i])
        for i, (part, (at, size)) in enumerate(zip(parts, pieces))
    ]
    term_copies = [
        copy(staged.at[pl.ds(at, size)], term, term_sem.at[i])
        for i, (term, (at, size)) in enumerate(zip(terms, term_pieces))
    ]
    grad_copies = [copy(kg_ref, kg_hbm, sem.at[4]), copy(vg_ref, vg_hbm, sem.at[5])]
    if last:
        late_copies = [
            copy(kg_in, kg_ref.at[:, pl.ds(0, HEAD)], sem.at[6]),
            copy(vg_in, vg_ref.at[:, pl.ds(0, HEAD)], sem.at[7]),
            copy(qg_in, qg_ref.at[pl.ds(0, 2 * HEAD)], sem.at[8]),
            copy(w_hbm, w_ref, sem.at[9]),
        ]
    else:
        late_copies = []
        table_copy = copy(meta_v, table, sem.at[6])
        grad_copies += [copy(qg_ref, qg_out, sem.at[7]), copy(meta_v, table_out, sem.at[8])]

    for c in far_copies + own_copies + late_copies:
        c.start()

    def clear(i, carry):
        acc[i] = jnp.zeros((2 * BLOCK, HEAD), F32)
        return carry

    lax.fori_loop(0, NX * nz + 1, clear, 0)
    for c in far_copies:
        c.wait()
    if not last:
        meta_v[...] = jnp.max(far[:, 2 * BLOCK :, :].astype(F32), axis=1).astype(jnp.int32)
        table_copy.start()
        table_copy.wait()
    for c in own_copies:
        c.wait()

    def node_step(node, carry):
        attend(
            h, node_count, nz, node, parents, lengths, spot, table, far, acc,
            q_ref, k_ref, v_ref, g_ref, kg_ref, vg_ref, qg_ref,
        )
        return carry

    lax.fori_loop(0, node_count, node_step, 0, unroll=UNROLL)

    def convert(i, carry):
        staged[i] = acc[i].astype(BF16)
        return carry

    lax.fori_loop(0, NX * nz, convert, 0)
    for c in term_copies:
        c.start()
    for c in late_copies:
        c.wait()
    for c in grad_copies:
        c.start()
    out_copies = []
    if last:
        tile = out_ref.shape[0] // TILES
        for i in range(TILES):
            at = slice(i * tile, (i + 1) * tile)
            out_ref[at, :] = dot(w_ref[at, :], qg_ref[...], 1, 0).astype(BF16)
            out_copies.append(copy(out_ref.at[at], out_hbm.at[at], out_sem.at[i]))
            out_copies[-1].start()
    for c in term_copies + grad_copies + out_copies:
        c.wait()


def attend(
    h, node_count, nz, node, parents, lengths, spot, table, far, acc,
    q_ref, k_ref, v_ref, g_ref, kg_ref, vg_ref, qg_ref,
):
    scale = QSCALAR ** (-0.5)
    x_me, z_me = spot[0], spot[1]
    here = pl.ds(pl.multiple_of(node * BLOCK, BLOCK), BLOCK)

    def place(link):
        safe = jnp.maximum(link, 0)
        lx = lax.div(safe, nz)
        sx = lax.rem(x_me - lx + NX, NX)
        sz = lax.rem(z_me - (safe - lx * nz) + nz, nz)
        return sx * nz + sz, sz * NX + sx

    parent = parents[node]
    link = jnp.where(parent >= 0, lax.div(jnp.maximum(parent, 0), node_count), -1)
    own_slot = jnp.where(node == 0, 0, NX * nz)
    slots, lens = [], [lengths[node]]
    for _ in range(3):
        both = place(link)
        slots.append(both[h])
        lens.append(jnp.where(link >= 0, table[both[0], 1], 0))
        link = jnp.where(link >= 0, table[both[0], 0], -1)

    cols = 2 * BLOCK
    key_row = lax.broadcasted_iota(jnp.int32, (BLOCK, cols), 0)
    query_col = lax.broadcasted_iota(jnp.int32, (BLOCK, cols), 1)
    query_col = jnp.where(query_col >= BLOCK, query_col - BLOCK, query_col)
    live = lax.broadcasted_iota(jnp.int32, (BLOCK, HEAD), 0) < lens[0]
    masks = [(key_row < lens[0]) & (key_row <= query_col)] + [key_row < m for m in lens[1:]]

    q = jnp.concatenate([q_ref[here, :HEAD], q_ref[here, HEAD:]], axis=0)
    zero = jnp.zeros((), BF16)
    g = jnp.concatenate(
        [jnp.where(live, g_ref[here, :HEAD], zero), jnp.where(live, g_ref[here, HEAD:], zero)], axis=0
    )
    at = slice(h * HEAD, (h + 1) * HEAD)
    keys = [k_ref[here, :]] + [far[s, 0:BLOCK, :] for s in slots]
    vals = [v_ref[here, :]] + [far[s, BLOCK : 2 * BLOCK, :] for s in slots]
    squash, weight, grad = [], [], []
    total = jnp.zeros((1, cols), F32)
    mixed = jnp.zeros((1, cols), F32)
    for b in range(4):
        t = jnp.tanh(dot(keys[b], q, 1, 1) * (scale / SOFTCAP))
        e = jnp.where(masks[b], jnp.exp(SOFTCAP * t), 0.0)
        d = dot(vals[b], g, 1, 1)
        total += jnp.sum(e, axis=0, keepdims=True)
        mixed += jnp.sum(e * d, axis=0, keepdims=True)
        squash.append(t)
        weight.append(e)
        grad.append(d)
    inverse = 1.0 / total
    delta = mixed * inverse
    query_grad = jnp.zeros((HEAD, cols), F32)
    for b in range(4):
        p = weight[b] * inverse
        ds = (p * (grad[b] - delta) * (scale - scale * (squash[b] * squash[b]))).astype(BF16)
        dk = dot(ds, q, 1, 0)
        dv = dot(p.astype(BF16), g, 1, 0)
        query_grad += dot(keys[b], ds, 0, 0)
        if b == 0:
            kg_ref[here, at] = dk.astype(BF16)
            vg_ref[here, at] = dv.astype(BF16)
        slot = slots[b - 1] if b else own_slot
        acc[slot, 0:BLOCK, :] += dk
        acc[slot, BLOCK:, :] += dv
    lo = 2 * h * HEAD
    qg_ref[lo : lo + HEAD, here] = query_grad[:, :BLOCK].astype(BF16)
    qg_ref[lo + HEAD : lo + 2 * HEAD, here] = query_grad[:, BLOCK:].astype(BF16)


def head_call(h, nz, pieces, term_pieces, scalars, arrays, extra, parts):
    last = h == 1
    queries, keys = arrays[:2]
    node_count = scalars[0].shape[0]
    rows, cols = queries.shape
    kv_cols = keys.shape[1]
    dp = NX * nz
    any_spec = pl.BlockSpec(memory_space=pl.ANY)
    smem = pl.BlockSpec(memory_space=pltpu.SMEM)
    wide = (h + 1) * HEAD
    far_rows = parts[0].shape[1]
    shape = jax.ShapeDtypeStruct
    out_shape = [shape((rows, wide), BF16)] * 2
    tail = []
    if last:
        width = extra[0].shape[0]
        out_shape += [shape((width, rows), BF16)]
        tail = [pltpu.VMEM((width, cols), BF16), pltpu.VMEM((width, rows), BF16)]
    else:
        out_shape += [shape((2 * wide, rows), BF16), shape((dp, HEAD), jnp.int32)]
        tail = [pltpu.VMEM((dp, HEAD), jnp.int32), pltpu.SMEM((dp, HEAD), jnp.int32)]
    out_shape += [shape((size, 2 * BLOCK, HEAD), BF16) for _, size in term_pieces]
    return pl.pallas_call(
        functools.partial(head_kernel, h, node_count, nz, pieces, term_pieces),
        in_specs=[smem] * len(scalars) + [any_spec] * (len(arrays) + len(extra) + len(parts)),
        out_specs=[any_spec] * len(out_shape),
        out_shape=out_shape,
        scratch_shapes=[
            pltpu.VMEM((rows, 2 * HEAD), BF16),
            pltpu.VMEM((rows, HEAD), BF16),
            pltpu.VMEM((rows, HEAD), BF16),
            pltpu.VMEM((rows, 2 * HEAD), BF16),
            pltpu.VMEM((rows, wide), BF16),
            pltpu.VMEM((rows, wide), BF16),
            pltpu.VMEM((2 * wide, rows), BF16),
            pltpu.VMEM((dp, far_rows, HEAD), BF16),
            pltpu.VMEM((dp + 1, 2 * BLOCK, HEAD), F32),
            pltpu.VMEM((dp, 2 * BLOCK, HEAD), BF16),
        ]
        + tail
        + [
            pltpu.SemaphoreType.DMA((10,)),
            pltpu.SemaphoreType.DMA((len(pieces),)),
            pltpu.SemaphoreType.DMA((len(term_pieces),)),
            pltpu.SemaphoreType.DMA((TILES,)),
        ],
        compiler_params=pltpu.CompilerParams(vmem_limit_bytes=58 * 1024 * 1024),
        name="second_head" if last else "first_head",
    )(*scalars, *arrays, *extra, *parts)


def local(queries, keys, values, out_grad, query_weight, parents, lengths, *, dp):
    node_count = parents.shape[0]
    kv_cols = keys.shape[1]
    nz = dp // NX
    half = nz // 2

    def send(array, dx, dz):
        pairs = [
            (x * nz + z, ((x + dx) % NX) * nz + (z + dz) % nz) for x in range(NX) for z in range(nz)
        ]
        return lax.ppermute(array, "dp", pairs)

    def add(*terms):
        return sum(t.astype(F32) for t in terms).astype(BF16)

    me = lax.axis_index("dp")
    spot = jnp.stack([me // nz, me % nz]).astype(jnp.int32)
    smem = pl.BlockSpec(memory_space=pltpu.SMEM)
    pack_a, pack_b = pl.pallas_call(
        functools.partial(pack_kernel, node_count),
        grid=(1,),
        in_specs=[smem, smem] + [pl.BlockSpec((BLOCK, kv_cols), lambda i: (0, 0))] * 2,
        out_specs=[
            pl.BlockSpec((2 * BLOCK + META, HEAD), lambda i: (0, 0)),
            pl.BlockSpec((2 * BLOCK, HEAD), lambda i: (0, 0)),
        ],
        out_shape=[
            jax.ShapeDtypeStruct((2 * BLOCK + META, HEAD), BF16),
            jax.ShapeDtypeStruct((2 * BLOCK, HEAD), BF16),
        ],
        name="pack",
    )(parents, lengths, keys, values)

    a1, a7, a2, a6 = (send(pack_a, 0, s) for s in (1, -1, 2, -2))
    b1, b3, b2 = (send(pack_b, s, 0) for s in (1, -1, 2))
    near_b = jnp.stack([pack_b, b1, b2, b3])
    a34 = send(jnp.stack([a1, a2]), 0, 2)
    a5 = send(a7, 0, -2)
    rings = [near_b] + [None] * (nz - 1)
    for s in range(1, half + 1):
        rings[s] = send(rings[s - 1], 0, 1)
        if s < half:
            rings[nz - s] = send(rings[(nz - s + 1) % nz], 0, -1)
    near_a = jnp.concatenate([jnp.stack([pack_a, a1, a2]), a34, jnp.stack([a5, a6, a7])])
    after, before = send(near_a, 1, 0), send(near_a, -1, 0)
    parts = [near_a, after, before, send(after[:half], 1, 0), send(before[half:], -1, 0)]

    arrays = (queries, keys, values, out_grad)
    five = [(0, nz), (nz, nz), (3 * nz, nz), (2 * nz, half), (2 * nz + half, half)]
    many = [(sz * NX, NX) for sz in range(nz)]
    pairs = [(at, half) for at in range(0, dp, half)]
    scalars = (parents, lengths, spot)
    kg, vg, qg, table, *terms = head_call(0, nz, five, pairs, scalars, arrays, (), parts)
    key_grad, value_grad, hidden, *more = head_call(
        1, nz, many, many, (*scalars, table), arrays, (query_weight, qg, kg, vg), rings
    )
    own, prev, far, succ = (terms[i : i + 2] for i in range(0, 2 * NX, 2))
    low_0, low_1 = send(far[0], -1, 0), send(prev[1], -1, 0)
    high_1, high_0 = send(far[1], 1, 0), send(succ[0], 1, 0)
    low_0, low_1, high_0, high_1, hidden, *more = lax.optimization_barrier(
        (low_0, low_1, high_0, high_1, hidden, *more)
    )

    hidden_grad = lax.psum_scatter(hidden, "tensor", scatter_dimension=0, tiled=True)

    low_0 = send(add(prev[0], low_0), -1, 0)
    high_1 = send(add(succ[1], high_1), 1, 0)
    low, high = send(more[half], 0, -1), send(more[half + 1], 0, 1)
    for s in range(half - 1, 0, -1):
        low = send(add(more[s], low), 0, -1)
    for s in range(half + 2, nz):
        high = send(add(more[s], high), 0, 1)
    line = [add(own[0][s], low_0[s], high_0[s]) for s in range(half)]
    line += [add(own[1][s], low_1[s], high_1[s]) for s in range(half)]
    s6 = send(line[6], 0, 2)
    s34 = send(jnp.stack(line[3:5]), 0, -2)
    s5 = send(line[5], 0, 2)
    s1 = send(add(line[1], s34[0]), 0, -1)
    s2 = send(add(line[2], s34[1]), 0, -2)
    s7 = send(add(line[7], s5), 0, 1)
    sum_a = add(line[0], s1, s2, s6, s7)
    line_b = [add(more[0][s], low[s], high[s]) for s in range(NX)]
    sum_b = add(line_b[0], *[send(line_b[s], -s, 0) for s in range(1, NX)])
    first_key = jnp.concatenate([sum_a[:BLOCK], sum_b[:BLOCK]], axis=1)
    first_value = jnp.concatenate([sum_a[BLOCK:], sum_b[BLOCK:]], axis=1)
    key_grad = lax.dynamic_update_slice(key_grad, first_key, (0, 0))
    value_grad = lax.dynamic_update_slice(value_grad, first_value, (0, 0))
    return (key_grad, value_grad, hidden_grad)


def solution(mesh):
    in_specs = (
        P("dp", "tensor"),
        P("dp", "tensor"),
        P("dp", "tensor"),
        P("dp", "tensor"),
        P(None, "tensor"),
        P("dp"),
        P("dp"),
    )
    out_specs = (P("dp", "tensor"), P("dp", "tensor"), P("tensor", "dp"))
    return jax.shard_map(
        functools.partial(local, dp=mesh.shape["dp"]),
        mesh=mesh,
        in_specs=in_specs,
        out_specs=out_specs,
        check_vma=False,
    )
```

```python
import functools

import jax
import jax.numpy as jnp
from jax import lax
from jax.experimental import pallas as pl
from jax.experimental.pallas import tpu as pltpu
from jax.sharding import PartitionSpec as P

HEAD = 128
SOFTCAP = 50
BLOCK = 128
QSCALAR = 144
META = 16
TILES = 6
UNROLL = 2
NX = 4
F32, BF16 = jnp.float32, jnp.bfloat16


def dot(a, b, ca, cb):
    return lax.dot_general(a, b, (((ca,), (cb,)), ((), ())), preferred_element_type=F32)


def pack_kernel(node_count, parents, lengths, k_ref, v_ref, a_ref, b_ref):
    a_ref[0:BLOCK] = k_ref[:, :HEAD]
    a_ref[BLOCK : 2 * BLOCK] = v_ref[:, :HEAD]
    b_ref[0:BLOCK] = k_ref[:, HEAD:]
    b_ref[BLOCK : 2 * BLOCK] = v_ref[:, HEAD:]
    parent = parents[0]
    link = jnp.where(parent >= 0, lax.div(jnp.maximum(parent, 0), node_count), -1)
    lane = lax.broadcasted_iota(jnp.int32, (META, HEAD), 1)
    meta = jnp.where(lane == 0, link, lengths[0])
    a_ref[2 * BLOCK :] = meta.astype(F32).astype(BF16)


def head_kernel(h, node_count, nz, pieces, parents, lengths, spot, *refs):
    last = h == 1
    if last:
        table, refs = refs[0], refs[1:]
    q_hbm, k_hbm, v_hbm, g_hbm, *refs = refs
    if last:
        w_hbm, qg_in, kg_in, vg_in, *refs = refs
    parts, refs = refs[: len(pieces)], refs[len(pieces) :]
    kg_hbm, vg_hbm, *refs = refs
    if last:
        out_hbm, *refs = refs
    else:
        qg_out, table_out, *refs = refs
    terms, refs = refs[: len(pieces)], refs[len(pieces) :]
    q_ref, k_ref, v_ref, g_ref, kg_ref, vg_ref, qg_ref, far, acc, staged, *refs = refs
    if last:
        w_ref, out_ref, *refs = refs
    else:
        meta_v, table, *refs = refs
    sem, far_sem, term_sem, out_sem = refs
    copy = pltpu.make_async_copy
    lines = pl.ds(h * HEAD, HEAD)
    pair = pl.ds(2 * h * HEAD, 2 * HEAD)
    own_copies = [
        copy(q_hbm.at[:, pair], q_ref, sem.at[0]),
        copy(k_hbm.at[:, lines], k_ref, sem.at[1]),
        copy(v_hbm.at[:, lines], v_ref, sem.at[2]),
        copy(g_hbm.at[:, pair], g_ref, sem.at[3]),
    ]
    far_copies = [
        copy(part, far.at[pl.ds(at, size)], far_sem.at[i])
        for i, (part, (at, size)) in enumerate(zip(parts, pieces))
    ]
    term_copies = [
        copy(staged.at[pl.ds(at, size)], term, term_sem.at[i])
        for i, (term, (at, size)) in enumerate(zip(terms, pieces))
    ]
    grad_copies = [copy(kg_ref, kg_hbm, sem.at[4]), copy(vg_ref, vg_hbm, sem.at[5])]
    if last:
        late_copies = [
            copy(kg_in, kg_ref.at[:, pl.ds(0, HEAD)], sem.at[6]),
            copy(vg_in, vg_ref.at[:, pl.ds(0, HEAD)], sem.at[7]),
            copy(qg_in, qg_ref.at[pl.ds(0, 2 * HEAD)], sem.at[8]),
            copy(w_hbm, w_ref, sem.at[9]),
        ]
    else:
        late_copies = []
        table_copy = copy(meta_v, table, sem.at[6])
        grad_copies += [copy(qg_ref, qg_out, sem.at[7]), copy(meta_v, table_out, sem.at[8])]

    for c in far_copies + own_copies + late_copies:
        c.start()

    def clear(i, carry):
        acc[i] = jnp.zeros((2 * BLOCK, HEAD), F32)
        return carry

    lax.fori_loop(0, NX * nz + 1, clear, 0)
    for c in far_copies:
        c.wait()
    if not last:
        meta_v[...] = jnp.max(far[:, 2 * BLOCK :, :].astype(F32), axis=1).astype(jnp.int32)
        table_copy.start()
        table_copy.wait()
    for c in own_copies:
        c.wait()

    def node_step(node, carry):
        attend(
            h, node_count, nz, node, parents, lengths, spot, table, far, acc,
            q_ref, k_ref, v_ref, g_ref, kg_ref, vg_ref, qg_ref,
        )
        return carry

    lax.fori_loop(0, node_count, node_step, 0, unroll=UNROLL)

    def convert(i, carry):
        staged[i] = acc[i].astype(BF16)
        return carry

    lax.fori_loop(0, NX * nz, convert, 0)
    for c in term_copies:
        c.start()
    for c in late_copies:
        c.wait()
    for c in grad_copies:
        c.start()
    if last:
        tile = out_ref.shape[0] // TILES

        def out_copy(i):
            at = pl.ds(pl.multiple_of(i * tile, tile), tile)
            return at, copy(out_ref.at[at], out_hbm.at[at], out_sem.at[i])

        def hidden_step(i, carry):
            at, tile_copy = out_copy(i)
            out_ref[at, :] = dot(w_ref[at, :], qg_ref[...], 1, 0).astype(BF16)
            tile_copy.start()
            return carry

        def hidden_wait(i, carry):
            out_copy(i)[1].wait()
            return carry

        lax.fori_loop(0, TILES, hidden_step, 0)
    for c in term_copies + grad_copies:
        c.wait()
    if last:
        lax.fori_loop(0, TILES, hidden_wait, 0)


def attend(
    h, node_count, nz, node, parents, lengths, spot, table, far, acc,
    q_ref, k_ref, v_ref, g_ref, kg_ref, vg_ref, qg_ref,
):
    scale = QSCALAR ** (-0.5)
    x_me, z_me = spot[0], spot[1]
    here = pl.ds(pl.multiple_of(node * BLOCK, BLOCK), BLOCK)

    def place(link):
        safe = jnp.maximum(link, 0)
        lx = lax.div(safe, nz)
        sx = lax.rem(x_me - lx + NX, NX)
        sz = lax.rem(z_me - (safe - lx * nz) + nz, nz)
        return sx * nz + sz, sz * NX + sx

    parent = parents[node]
    link = jnp.where(parent >= 0, lax.div(jnp.maximum(parent, 0), node_count), -1)
    own_slot = jnp.where(node == 0, 0, NX * nz)
    slots, lens = [], [lengths[node]]
    for _ in range(3):
        both = place(link)
        slots.append(both[h])
        lens.append(jnp.where(link >= 0, table[both[0], 1], 0))
        link = jnp.where(link >= 0, table[both[0], 0], -1)

    cols = 2 * BLOCK
    key_row = lax.broadcasted_iota(jnp.int32, (BLOCK, cols), 0)
    query_col = lax.broadcasted_iota(jnp.int32, (BLOCK, cols), 1)
    query_col = jnp.where(query_col >= BLOCK, query_col - BLOCK, query_col)
    live = lax.broadcasted_iota(jnp.int32, (BLOCK, HEAD), 0) < lens[0]
    masks = [(key_row < lens[0]) & (key_row <= query_col)] + [key_row < m for m in lens[1:]]

    q = jnp.concatenate([q_ref[here, :HEAD], q_ref[here, HEAD:]], axis=0)
    zero = jnp.zeros((), BF16)
    g = jnp.concatenate(
        [jnp.where(live, g_ref[here, :HEAD], zero), jnp.where(live, g_ref[here, HEAD:], zero)], axis=0
    )
    at = slice(h * HEAD, (h + 1) * HEAD)
    keys = [k_ref[here, :]] + [far[s, 0:BLOCK, :] for s in slots]
    vals = [v_ref[here, :]] + [far[s, BLOCK : 2 * BLOCK, :] for s in slots]
    squash, weight, grad = [], [], []
    total = jnp.zeros((1, cols), F32)
    mixed = jnp.zeros((1, cols), F32)
    for b in range(4):
        t = jnp.tanh(dot(keys[b], q, 1, 1) * (scale / SOFTCAP))
        e = jnp.where(masks[b], jnp.exp(SOFTCAP * t), 0.0)
        d = dot(vals[b], g, 1, 1)
        total += jnp.sum(e, axis=0, keepdims=True)
        mixed += jnp.sum(e * d, axis=0, keepdims=True)
        squash.append(t)
        weight.append(e)
        grad.append(d)
    inverse = 1.0 / total
    delta = mixed * inverse
    query_grad = jnp.zeros((HEAD, cols), F32)
    for b in range(4):
        p = weight[b] * inverse
        ds = (p * (grad[b] - delta) * (scale - scale * (squash[b] * squash[b]))).astype(BF16)
        dk = dot(ds, q, 1, 0)
        dv = dot(p.astype(BF16), g, 1, 0)
        query_grad += dot(keys[b], ds, 0, 0)
        if b == 0:
            kg_ref[here, at] = dk.astype(BF16)
            vg_ref[here, at] = dv.astype(BF16)
        slot = slots[b - 1] if b else own_slot
        acc[slot, 0:BLOCK, :] += dk
        acc[slot, BLOCK:, :] += dv
    lo = 2 * h * HEAD
    qg_ref[lo : lo + HEAD, here] = query_grad[:, :BLOCK].astype(BF16)
    qg_ref[lo + HEAD : lo + 2 * HEAD, here] = query_grad[:, BLOCK:].astype(BF16)


def head_call(h, nz, pieces, scalars, arrays, extra, parts):
    last = h == 1
    queries, keys = arrays[:2]
    node_count = scalars[0].shape[0]
    rows, cols = queries.shape
    kv_cols = keys.shape[1]
    dp = NX * nz
    any_spec = pl.BlockSpec(memory_space=pl.ANY)
    smem = pl.BlockSpec(memory_space=pltpu.SMEM)
    wide = (h + 1) * HEAD
    far_rows = parts[0].shape[1]
    shape = jax.ShapeDtypeStruct
    out_shape = [shape((rows, wide), BF16)] * 2
    tail = []
    if last:
        width = extra[0].shape[0]
        out_shape += [shape((width, rows), BF16)]
        tail = [pltpu.VMEM((width, cols), BF16), pltpu.VMEM((width, rows), BF16)]
    else:
        out_shape += [shape((2 * wide, rows), BF16), shape((dp, HEAD), jnp.int32)]
        tail = [pltpu.VMEM((dp, HEAD), jnp.int32), pltpu.SMEM((dp, HEAD), jnp.int32)]
    out_shape += [shape((size, 2 * BLOCK, HEAD), BF16) for _, size in pieces]
    return pl.pallas_call(
        functools.partial(head_kernel, h, node_count, nz, pieces),
        in_specs=[smem] * len(scalars) + [any_spec] * (len(arrays) + len(extra) + len(parts)),
        out_specs=[any_spec] * len(out_shape),
        out_shape=out_shape,
        scratch_shapes=[
            pltpu.VMEM((rows, 2 * HEAD), BF16),
            pltpu.VMEM((rows, HEAD), BF16),
            pltpu.VMEM((rows, HEAD), BF16),
            pltpu.VMEM((rows, 2 * HEAD), BF16),
            pltpu.VMEM((rows, wide), BF16),
            pltpu.VMEM((rows, wide), BF16),
            pltpu.VMEM((2 * wide, rows), BF16),
            pltpu.VMEM((dp, far_rows, HEAD), BF16),
            pltpu.VMEM((dp + 1, 2 * BLOCK, HEAD), F32),
            pltpu.VMEM((dp, 2 * BLOCK, HEAD), BF16),
        ]
        + tail
        + [
            pltpu.SemaphoreType.DMA((10,)),
            pltpu.SemaphoreType.DMA((len(pieces),)),
            pltpu.SemaphoreType.DMA((len(pieces),)),
            pltpu.SemaphoreType.DMA((TILES,)),
        ],
        compiler_params=pltpu.CompilerParams(vmem_limit_bytes=58 * 1024 * 1024),
        name="second_head" if last else "first_head",
    )(*scalars, *arrays, *extra, *parts)


def main_calls(nz, parents, lengths, spot, queries, keys, values, out_grad, query_weight, parts):
    half = nz // 2
    arrays = (queries, keys, values, out_grad)
    pieces_a = [(0, nz), (nz, nz), (3 * nz, nz), (2 * nz, half), (2 * nz + half, half)]
    pieces_b = [(sz * NX, NX) for sz in range(nz)]
    kg, vg, qg, table, *terms_a = head_call(
        0, nz, pieces_a, (parents, lengths, spot), arrays, (), parts[:5]
    )
    key_grad, value_grad, hidden, *terms_b = head_call(
        1, nz, pieces_b, (parents, lengths, spot, table), arrays, (query_weight, qg, kg, vg), parts[5:]
    )
    return (key_grad, value_grad, hidden, *terms_a, *terms_b)


def local(queries, keys, values, out_grad, query_weight, parents, lengths, *, dp):
    node_count = parents.shape[0]
    kv_cols = keys.shape[1]
    nz = dp // NX
    half = nz // 2

    def send(array, dx, dz):
        pairs = [
            (x * nz + z, ((x + dx) % NX) * nz + (z + dz) % nz) for x in range(NX) for z in range(nz)
        ]
        return lax.ppermute(array, "dp", pairs)

    def add(*terms):
        return sum(t.astype(F32) for t in terms).astype(BF16)

    me = lax.axis_index("dp")
    spot = jnp.stack([me // nz, me % nz]).astype(jnp.int32)
    smem = pl.BlockSpec(memory_space=pltpu.SMEM)
    pack_a, pack_b = pl.pallas_call(
        functools.partial(pack_kernel, node_count),
        grid=(1,),
        in_specs=[smem, smem] + [pl.BlockSpec((BLOCK, kv_cols), lambda i: (0, 0))] * 2,
        out_specs=[
            pl.BlockSpec((2 * BLOCK + META, HEAD), lambda i: (0, 0)),
            pl.BlockSpec((2 * BLOCK, HEAD), lambda i: (0, 0)),
        ],
        out_shape=[
            jax.ShapeDtypeStruct((2 * BLOCK + META, HEAD), BF16),
            jax.ShapeDtypeStruct((2 * BLOCK, HEAD), BF16),
        ],
        name="pack",
    )(parents, lengths, keys, values)

    a1, a7, a2, a6 = (send(pack_a, 0, s) for s in (1, -1, 2, -2))
    b1, b3, b2 = (send(pack_b, s, 0) for s in (1, -1, 2))
    near_b = jnp.stack([pack_b, b1, b2, b3])
    a34 = send(jnp.stack([a1, a2]), 0, 2)
    a5 = send(a7, 0, -2)
    rings = [near_b] + [None] * (nz - 1)
    for s in range(1, half + 1):
        rings[s] = send(rings[s - 1], 0, 1)
        if s < half:
            rings[nz - s] = send(rings[(nz - s + 1) % nz], 0, -1)
    near_a = jnp.concatenate([jnp.stack([pack_a, a1, a2]), a34, jnp.stack([a5, a6, a7])])
    after, before = send(near_a, 1, 0), send(near_a, -1, 0)
    parts = [near_a, after, before, send(after[:half], 1, 0), send(before[half:], -1, 0)] + rings

    outs = main_calls(nz, parents, lengths, spot, queries, keys, values, out_grad, query_weight, parts)
    key_grad, value_grad, hidden = outs[:3]
    own, prev, succ, far_low, far_high = outs[3:8]
    terms = outs[8:]

    hidden_grad = lax.psum_scatter(hidden, "tensor", scatter_dimension=0, tiled=True)

    low_a, high_a = send(far_low, -1, 0), send(far_high, 1, 0)
    low, high = send(terms[half], 0, -1), send(terms[half + 1], 0, 1)
    low_a = send(jnp.concatenate([add(prev[:half], low_a), prev[half:]]), -1, 0)
    high_a = send(jnp.concatenate([succ[:half], add(succ[half:], high_a)]), 1, 0)
    for s in range(half - 1, 0, -1):
        low = send(add(terms[s], low), 0, -1)
    for s in range(half + 2, nz):
        high = send(add(terms[s], high), 0, 1)
    line = [add(own[s], low_a[s], high_a[s]) for s in range(nz)]
    s6 = send(line[6], 0, 2)
    s34 = send(jnp.stack(line[3:5]), 0, -2)
    s5 = send(line[5], 0, 2)
    s1 = send(add(line[1], s34[0]), 0, -1)
    s2 = send(add(line[2], s34[1]), 0, -2)
    s7 = send(add(line[7], s5), 0, 1)
    sum_a = add(line[0], s1, s2, s6, s7)
    line_b = [add(terms[0][s], low[s], high[s]) for s in range(NX)]
    sum_b = add(line_b[0], *[send(line_b[s], -s, 0) for s in range(1, NX)])
    first_key = jnp.concatenate([sum_a[:BLOCK], sum_b[:BLOCK]], axis=1)
    first_value = jnp.concatenate([sum_a[BLOCK:], sum_b[BLOCK:]], axis=1)
    key_grad = lax.dynamic_update_slice(key_grad, first_key, (0, 0))
    value_grad = lax.dynamic_update_slice(value_grad, first_value, (0, 0))
    return (key_grad, value_grad, hidden_grad)


def solution(mesh):
    in_specs = (
        P("dp", "tensor"),
        P("dp", "tensor"),
        P("dp", "tensor"),
        P("dp", "tensor"),
        P(None, "tensor"),
        P("dp"),
        P("dp"),
    )
    out_specs = (P("dp", "tensor"), P("dp", "tensor"), P("tensor", "dp"))
    return jax.shard_map(
        functools.partial(local, dp=mesh.shape["dp"]),
        mesh=mesh,
        in_specs=in_specs,
        out_specs=out_specs,
        check_vma=False,
    )
```

```python
import functools

import jax
import jax.numpy as jnp
from jax import lax
from jax.experimental import pallas as pl
from jax.experimental.pallas import tpu as pltpu
from jax.sharding import PartitionSpec as P

HEAD = 128
SOFTCAP = 50
BLOCK = 128
QSCALAR = 144
META = 16
TILES = 6
UNROLL = 1
NX = 4
F32, BF16 = jnp.float32, jnp.bfloat16


def dot(a, b, ca, cb):
    return lax.dot_general(a, b, (((ca,), (cb,)), ((), ())), preferred_element_type=F32)


def pack_kernel(node_count, parents, lengths, k_ref, v_ref, a_ref, b_ref):
    a_ref[0:BLOCK] = k_ref[:, :HEAD]
    a_ref[BLOCK : 2 * BLOCK] = v_ref[:, :HEAD]
    b_ref[0:BLOCK] = k_ref[:, HEAD:]
    b_ref[BLOCK : 2 * BLOCK] = v_ref[:, HEAD:]
    parent = parents[0]
    link = jnp.where(parent >= 0, lax.div(jnp.maximum(parent, 0), node_count), -1)
    lane = lax.broadcasted_iota(jnp.int32, (META, HEAD), 1)
    meta = jnp.where(lane == 0, link, lengths[0])
    a_ref[2 * BLOCK :] = meta.astype(F32).astype(BF16)


def main_kernel(node_count, nz, parents, lengths, spot, q_hbm, k_hbm, v_hbm, g_hbm, w_hbm, *refs):
    parts, refs = refs[: 5 + nz], refs[5 + nz :]
    kg_hbm, vg_hbm, out_hbm = refs[:3]
    terms, refs = refs[3 : 8 + nz], refs[8 + nz :]
    q_ref, k_ref, v_ref, g_ref, w_ref, kg_ref, vg_ref, qg_ref, out_ref, *refs = refs
    far_a, far_b, acc_a, acc_b, send_a, send_b, meta_v, meta_s, *sems = refs
    own_sem, far_sem, term_sem, grad_sem, out_sem, one_sem = sems
    half = nz // 2
    pieces = [(0, nz), (nz, nz), (3 * nz, nz), (2 * nz, half), (2 * nz + half, half)]
    ranges = [(0, at, size) for at, size in pieces] + [(1, sz * NX, NX) for sz in range(nz)]
    own_pairs = [(q_hbm, q_ref), (k_hbm, k_ref), (v_hbm, v_ref), (g_hbm, g_ref)]
    own_copies = [pltpu.make_async_copy(a, b, own_sem.at[i]) for i, (a, b) in enumerate(own_pairs)]
    far_copies = [
        pltpu.make_async_copy(part, (far_a, far_b)[h].at[pl.ds(at, size)], far_sem.at[i])
        for i, (part, (h, at, size)) in enumerate(zip(parts, ranges))
    ]
    term_copies = [
        pltpu.make_async_copy((send_a, send_b)[h].at[pl.ds(at, size)], term, term_sem.at[i])
        for i, (term, (h, at, size)) in enumerate(zip(terms, ranges))
    ]
    grad_copies = [
        pltpu.make_async_copy(kg_ref, kg_hbm, grad_sem.at[0]),
        pltpu.make_async_copy(vg_ref, vg_hbm, grad_sem.at[1]),
    ]
    weight_copy = pltpu.make_async_copy(w_hbm, w_ref, one_sem.at[0])
    meta_copy = pltpu.make_async_copy(meta_v, meta_s, one_sem.at[1])

    for copy in far_copies + own_copies + [weight_copy]:
        copy.start()

    def clear(i, carry):
        acc_a[i] = jnp.zeros((2 * BLOCK, HEAD), F32)
        acc_b[i] = jnp.zeros((2 * BLOCK, HEAD), F32)
        return carry

    lax.fori_loop(0, NX * nz + 1, clear, 0)
    for copy in far_copies:
        copy.wait()
    meta_v[...] = jnp.max(far_a[:, 2 * BLOCK :, :].astype(F32), axis=1).astype(jnp.int32)
    meta_copy.start()
    for copy in own_copies:
        copy.wait()
    meta_copy.wait()

    def node_step(node, carry):
        attend(
            node_count, nz, node, parents, lengths, spot, meta_s, (far_a, far_b), (acc_a, acc_b),
            q_ref, k_ref, v_ref, g_ref, kg_ref, vg_ref, qg_ref,
        )
        return carry

    lax.fori_loop(0, node_count, node_step, 0, unroll=UNROLL)

    def convert(i, carry):
        send_a[i] = acc_a[i].astype(BF16)
        send_b[i] = acc_b[i].astype(BF16)
        return carry

    lax.fori_loop(0, NX * nz, convert, 0)
    for copy in term_copies + grad_copies:
        copy.start()
    weight_copy.wait()
    tile = out_ref.shape[0] // TILES

    def out_copy(i):
        at = pl.ds(pl.multiple_of(i * tile, tile), tile)
        return at, pltpu.make_async_copy(out_ref.at[at], out_hbm.at[at], out_sem.at[i])

    def hidden_step(i, carry):
        at, tile_copy = out_copy(i)
        out_ref[at, :] = dot(w_ref[at, :], qg_ref[...], 1, 0).astype(BF16)
        tile_copy.start()
        return carry

    def hidden_wait(i, carry):
        out_copy(i)[1].wait()
        return carry

    lax.fori_loop(0, TILES, hidden_step, 0)
    for copy in term_copies + grad_copies:
        copy.wait()
    lax.fori_loop(0, TILES, hidden_wait, 0)


def attend(
    node_count, nz, node, parents, lengths, spot, meta_s, far_refs, acc_refs,
    q_ref, k_ref, v_ref, g_ref, kg_ref, vg_ref, qg_ref,
):
    scale = QSCALAR ** (-0.5)
    x_me, z_me = spot[0], spot[1]
    here = pl.ds(pl.multiple_of(node * BLOCK, BLOCK), BLOCK)

    def place(link):
        safe = jnp.maximum(link, 0)
        lx = lax.div(safe, nz)
        sx = lax.rem(x_me - lx + NX, NX)
        sz = lax.rem(z_me - (safe - lx * nz) + nz, nz)
        return sx * nz + sz, sz * NX + sx

    parent = parents[node]
    link = jnp.where(parent >= 0, lax.div(jnp.maximum(parent, 0), node_count), -1)
    slots, lens = [], [lengths[node]]
    own_slot = jnp.where(node == 0, 0, NX * nz)
    for _ in range(3):
        slot_a, slot_b = place(link)
        slots.append((slot_a, slot_b))
        lens.append(jnp.where(link >= 0, meta_s[slot_a, 1], 0))
        link = jnp.where(link >= 0, meta_s[slot_a, 0], -1)

    cols = 2 * BLOCK
    key_row = lax.broadcasted_iota(jnp.int32, (BLOCK, cols), 0)
    query_col = lax.broadcasted_iota(jnp.int32, (BLOCK, cols), 1)
    query_col = jnp.where(query_col >= BLOCK, query_col - BLOCK, query_col)
    live = lax.broadcasted_iota(jnp.int32, (BLOCK, HEAD), 0) < lens[0]
    masks = [(key_row < lens[0]) & (key_row <= query_col)] + [key_row < m for m in lens[1:]]

    for h in range(2):
        far = far_refs[h]
        acc = acc_refs[h]
        lo, mid, hi = 2 * h * HEAD, (2 * h + 1) * HEAD, (2 * h + 2) * HEAD
        q = jnp.concatenate([q_ref[here, lo:mid], q_ref[here, mid:hi]], axis=0)
        zero = jnp.zeros((), BF16)
        g = jnp.concatenate(
            [jnp.where(live, g_ref[here, lo:mid], zero), jnp.where(live, g_ref[here, mid:hi], zero)], axis=0
        )
        at = slice(h * HEAD, (h + 1) * HEAD)
        keys = [k_ref[here, at]] + [far[s[h], 0:BLOCK, :] for s in slots]
        vals = [v_ref[here, at]] + [far[s[h], BLOCK : 2 * BLOCK, :] for s in slots]
        squash, weight, grad = [], [], []
        total = jnp.zeros((1, cols), F32)
        mixed = jnp.zeros((1, cols), F32)
        for b in range(4):
            t = jnp.tanh(dot(keys[b], q, 1, 1) * (scale / SOFTCAP))
            e = jnp.where(masks[b], jnp.exp(SOFTCAP * t), 0.0)
            d = dot(vals[b], g, 1, 1)
            total += jnp.sum(e, axis=0, keepdims=True)
            mixed += jnp.sum(e * d, axis=0, keepdims=True)
            squash.append(t)
            weight.append(e)
            grad.append(d)
        inverse = 1.0 / total
        delta = mixed * inverse
        query_grad = jnp.zeros((HEAD, cols), F32)
        for b in range(4):
            p = weight[b] * inverse
            ds = (p * (grad[b] - delta) * (scale - scale * (squash[b] * squash[b]))).astype(BF16)
            dk = dot(ds, q, 1, 0)
            dv = dot(p.astype(BF16), g, 1, 0)
            query_grad += dot(keys[b], ds, 0, 0)
            if b == 0:
                kg_ref[here, at] = dk.astype(BF16)
                vg_ref[here, at] = dv.astype(BF16)

            slot = slots[b - 1][h] if b else own_slot
            acc[slot, 0:BLOCK, :] += dk
            acc[slot, BLOCK:, :] += dv
        qg_ref[lo:mid, here] = query_grad[:, :BLOCK].astype(BF16)
        qg_ref[mid:hi, here] = query_grad[:, BLOCK:].astype(BF16)


def main_call(nz, parents, lengths, spot, queries, keys, values, out_grad, query_weight, parts):
    node_count = parents.shape[0]
    rows, cols = queries.shape
    kv_cols = keys.shape[1]
    width = query_weight.shape[0]
    dp = NX * nz
    half = nz // 2
    any_spec = pl.BlockSpec(memory_space=pl.ANY)
    smem = pl.BlockSpec(memory_space=pltpu.SMEM)
    sizes = [nz, nz, nz, half, half] + [NX] * nz
    return pl.pallas_call(
        functools.partial(main_kernel, node_count, nz),
        in_specs=[smem] * 3 + [any_spec] * (10 + nz),
        out_specs=[any_spec] * (8 + nz),
        out_shape=[
            jax.ShapeDtypeStruct((rows, kv_cols), BF16),
            jax.ShapeDtypeStruct((rows, kv_cols), BF16),
            jax.ShapeDtypeStruct((width, rows), BF16),
        ]
        + [jax.ShapeDtypeStruct((size, 2 * BLOCK, HEAD), BF16) for size in sizes],
        scratch_shapes=[
            pltpu.VMEM((rows, cols), BF16),
            pltpu.VMEM((rows, kv_cols), BF16),
            pltpu.VMEM((rows, kv_cols), BF16),
            pltpu.VMEM((rows, cols), BF16),
            pltpu.VMEM((width, cols), BF16),
            pltpu.VMEM((rows, kv_cols), BF16),
            pltpu.VMEM((rows, kv_cols), BF16),
            pltpu.VMEM((cols, rows), BF16),
            pltpu.VMEM((width, rows), BF16),
            pltpu.VMEM((dp, 2 * BLOCK + META, HEAD), BF16),
            pltpu.VMEM((dp, 2 * BLOCK, HEAD), BF16),
            pltpu.VMEM((dp + 1, 2 * BLOCK, HEAD), F32),
            pltpu.VMEM((dp + 1, 2 * BLOCK, HEAD), F32),
            pltpu.VMEM((dp, 2 * BLOCK, HEAD), BF16),
            pltpu.VMEM((dp, 2 * BLOCK, HEAD), BF16),
            pltpu.VMEM((dp, HEAD), jnp.int32),
            pltpu.SMEM((dp, HEAD), jnp.int32),
            pltpu.SemaphoreType.DMA((4,)),
            pltpu.SemaphoreType.DMA((5 + nz,)),
            pltpu.SemaphoreType.DMA((5 + nz,)),
            pltpu.SemaphoreType.DMA((2,)),
            pltpu.SemaphoreType.DMA((TILES,)),
            pltpu.SemaphoreType.DMA((2,)),
        ],
        compiler_params=pltpu.CompilerParams(vmem_limit_bytes=58 * 1024 * 1024),
        name="attention",
    )(parents, lengths, spot, queries, keys, values, out_grad, query_weight, *parts)


def local(queries, keys, values, out_grad, query_weight, parents, lengths, *, dp):
    node_count = parents.shape[0]
    kv_cols = keys.shape[1]
    nz = dp // NX
    half = nz // 2

    def send(array, dx, dz):
        pairs = [
            (x * nz + z, ((x + dx) % NX) * nz + (z + dz) % nz) for x in range(NX) for z in range(nz)
        ]
        return lax.ppermute(array, "dp", pairs)

    def add(*terms):
        return sum(t.astype(F32) for t in terms).astype(BF16)

    me = lax.axis_index("dp")
    spot = jnp.stack([me // nz, me % nz]).astype(jnp.int32)
    smem = pl.BlockSpec(memory_space=pltpu.SMEM)
    pack_a, pack_b = pl.pallas_call(
        functools.partial(pack_kernel, node_count),
        grid=(1,),
        in_specs=[smem, smem] + [pl.BlockSpec((BLOCK, kv_cols), lambda i: (0, 0))] * 2,
        out_specs=[
            pl.BlockSpec((2 * BLOCK + META, HEAD), lambda i: (0, 0)),
            pl.BlockSpec((2 * BLOCK, HEAD), lambda i: (0, 0)),
        ],
        out_shape=[
            jax.ShapeDtypeStruct((2 * BLOCK + META, HEAD), BF16),
            jax.ShapeDtypeStruct((2 * BLOCK, HEAD), BF16),
        ],
        name="pack",
    )(parents, lengths, keys, values)

    a1, a7, a2, a6 = (send(pack_a, 0, s) for s in (1, -1, 2, -2))
    b1, b3, b2 = (send(pack_b, s, 0) for s in (1, -1, 2))
    near_b = jnp.stack([pack_b, b1, b2, b3])
    a34 = send(jnp.stack([a1, a2]), 0, 2)
    a5 = send(a7, 0, -2)
    rings = [near_b] + [None] * (nz - 1)
    for s in range(1, half + 1):
        rings[s] = send(rings[s - 1], 0, 1)
        if s < half:
            rings[nz - s] = send(rings[(nz - s + 1) % nz], 0, -1)
    near_a = jnp.concatenate([jnp.stack([pack_a, a1, a2]), a34, jnp.stack([a5, a6, a7])])
    after, before = send(near_a, 1, 0), send(near_a, -1, 0)
    parts = [near_a, after, before, send(after[:half], 1, 0), send(before[half:], -1, 0)] + rings

    outs = main_call(nz, parents, lengths, spot, queries, keys, values, out_grad, query_weight, parts)
    key_grad, value_grad, hidden = outs[:3]
    own, prev, succ, far_low, far_high = outs[3:8]
    terms = outs[8:]

    hidden_grad = lax.psum_scatter(hidden, "tensor", scatter_dimension=0, tiled=True)

    low_a, high_a = send(far_low, -1, 0), send(far_high, 1, 0)
    low, high = send(terms[half], 0, -1), send(terms[half + 1], 0, 1)
    low_a = send(jnp.concatenate([add(prev[:half], low_a), prev[half:]]), -1, 0)
    high_a = send(jnp.concatenate([succ[:half], add(succ[half:], high_a)]), 1, 0)
    for s in range(half - 1, 0, -1):
        low = send(add(terms[s], low), 0, -1)
    for s in range(half + 2, nz):
        high = send(add(terms[s], high), 0, 1)
    line = [add(own[s], low_a[s], high_a[s]) for s in range(nz)]
    s6 = send(line[6], 0, 2)
    s34 = send(jnp.stack(line[3:5]), 0, -2)
    s5 = send(line[5], 0, 2)
    s1 = send(add(line[1], s34[0]), 0, -1)
    s2 = send(add(line[2], s34[1]), 0, -2)
    s7 = send(add(line[7], s5), 0, 1)
    sum_a = add(line[0], s1, s2, s6, s7)
    line_b = [add(terms[0][s], low[s], high[s]) for s in range(NX)]
    sum_b = add(line_b[0], *[send(line_b[s], -s, 0) for s in range(1, NX)])
    first_key = jnp.concatenate([sum_a[:BLOCK], sum_b[:BLOCK]], axis=1)
    first_value = jnp.concatenate([sum_a[BLOCK:], sum_b[BLOCK:]], axis=1)
    key_grad = lax.dynamic_update_slice(key_grad, first_key, (0, 0))
    value_grad = lax.dynamic_update_slice(value_grad, first_value, (0, 0))
    return (key_grad, value_grad, hidden_grad)


def solution(mesh):
    in_specs = (
        P("dp", "tensor"),
        P("dp", "tensor"),
        P("dp", "tensor"),
        P("dp", "tensor"),
        P(None, "tensor"),
        P("dp"),
        P("dp"),
    )
    out_specs = (P("dp", "tensor"), P("dp", "tensor"), P("tensor", "dp"))
    return jax.shard_map(
        functools.partial(local, dp=mesh.shape["dp"]),
        mesh=mesh,
        in_specs=in_specs,
        out_specs=out_specs,
        check_vma=False,
    )
```

```python
import functools

import jax
import jax.numpy as jnp
from jax import lax
from jax.experimental import pallas as pl
from jax.experimental.pallas import tpu as pltpu
from jax.sharding import PartitionSpec as P

HEAD = 128
SOFTCAP = 50
BLOCK = 128
QSCALAR = 144
META = 16
TILES = 6
UNROLL = 1
NX = 4
F32, BF16 = jnp.float32, jnp.bfloat16


def dot(a, b, ca, cb):
    return lax.dot_general(a, b, (((ca,), (cb,)), ((), ())), preferred_element_type=F32)


def pack_kernel(node_count, parents, lengths, k_ref, v_ref, a_ref, b_ref):
    a_ref[0:BLOCK] = k_ref[:, :HEAD]
    a_ref[BLOCK : 2 * BLOCK] = v_ref[:, :HEAD]
    b_ref[0:BLOCK] = k_ref[:, HEAD:]
    b_ref[BLOCK : 2 * BLOCK] = v_ref[:, HEAD:]
    parent = parents[0]
    link = jnp.where(parent >= 0, lax.div(jnp.maximum(parent, 0), node_count), -1)
    lane = lax.broadcasted_iota(jnp.int32, (META, HEAD), 1)
    meta = jnp.where(lane == 0, link, lengths[0])
    a_ref[2 * BLOCK :] = meta.astype(F32).astype(BF16)


def main_kernel(node_count, nz, parents, lengths, spot, q_hbm, k_hbm, v_hbm, g_hbm, w_hbm, *refs):
    parts, refs = refs[: 5 + nz], refs[5 + nz :]
    kg_hbm, vg_hbm, out_hbm = refs[:3]
    terms, refs = refs[3 : 8 + nz], refs[8 + nz :]
    q_ref, k_ref, v_ref, g_ref, w_ref, kg_ref, vg_ref, qg_ref, out_ref, *refs = refs
    far_a, far_b, acc_a, acc_b, send_a, send_b, meta_v, meta_s, *sems = refs
    own_sem, far_sem, term_sem, grad_sem, out_sem, one_sem = sems
    half = nz // 2
    pieces = [(0, nz), (nz, nz), (3 * nz, nz), (2 * nz, half), (2 * nz + half, half)]
    ranges = [(0, at, size) for at, size in pieces] + [(1, sz * NX, NX) for sz in range(nz)]
    own_pairs = [(q_hbm, q_ref), (k_hbm, k_ref), (v_hbm, v_ref), (g_hbm, g_ref)]
    own_copies = [pltpu.make_async_copy(a, b, own_sem.at[i]) for i, (a, b) in enumerate(own_pairs)]
    far_copies = [
        pltpu.make_async_copy(part, (far_a, far_b)[h].at[pl.ds(at, size)], far_sem.at[i])
        for i, (part, (h, at, size)) in enumerate(zip(parts, ranges))
    ]
    term_copies = [
        pltpu.make_async_copy((send_a, send_b)[h].at[pl.ds(at, size)], term, term_sem.at[i])
        for i, (term, (h, at, size)) in enumerate(zip(terms, ranges))
    ]
    grad_copies = [
        pltpu.make_async_copy(kg_ref, kg_hbm, grad_sem.at[0]),
        pltpu.make_async_copy(vg_ref, vg_hbm, grad_sem.at[1]),
    ]
    weight_copy = pltpu.make_async_copy(w_hbm, w_ref, one_sem.at[0])
    meta_copy = pltpu.make_async_copy(meta_v, meta_s, one_sem.at[1])

    for copy in far_copies + own_copies + [weight_copy]:
        copy.start()

    def clear(i, carry):
        acc_a[i] = jnp.zeros((2 * BLOCK, HEAD), F32)
        acc_b[i] = jnp.zeros((2 * BLOCK, HEAD), F32)
        return carry

    lax.fori_loop(0, NX * nz + 1, clear, 0)
    for copy in far_copies:
        copy.wait()
    meta_v[...] = jnp.max(far_a[:, 2 * BLOCK :, :].astype(F32), axis=1).astype(jnp.int32)
    meta_copy.start()
    for copy in own_copies:
        copy.wait()
    meta_copy.wait()

    def node_step(node, carry):
        attend(
            node_count, nz, node, parents, lengths, spot, meta_s, (far_a, far_b), (acc_a, acc_b),
            q_ref, k_ref, v_ref, g_ref, kg_ref, vg_ref, qg_ref,
        )
        return carry

    lax.fori_loop(0, node_count, node_step, 0, unroll=UNROLL)

    def convert(i, carry):
        send_a[i] = acc_a[i].astype(BF16)
        send_b[i] = acc_b[i].astype(BF16)
        return carry

    lax.fori_loop(0, NX * nz, convert, 0)
    for copy in term_copies + grad_copies:
        copy.start()
    weight_copy.wait()
    tile = out_ref.shape[0] // TILES

    def out_copy(i):
        at = pl.ds(pl.multiple_of(i * tile, tile), tile)
        return at, pltpu.make_async_copy(out_ref.at[at], out_hbm.at[at], out_sem.at[i])

    def hidden_step(i, carry):
        at, tile_copy = out_copy(i)
        out_ref[at, :] = dot(w_ref[at, :], qg_ref[...], 1, 0).astype(BF16)
        tile_copy.start()
        return carry

    def hidden_wait(i, carry):
        out_copy(i)[1].wait()
        return carry

    lax.fori_loop(0, TILES, hidden_step, 0)
    for copy in term_copies + grad_copies:
        copy.wait()
    lax.fori_loop(0, TILES, hidden_wait, 0)


def attend(
    node_count, nz, node, parents, lengths, spot, meta_s, far_refs, acc_refs,
    q_ref, k_ref, v_ref, g_ref, kg_ref, vg_ref, qg_ref,
):
    scale = QSCALAR ** (-0.5)
    x_me, z_me = spot[0], spot[1]
    here = pl.ds(pl.multiple_of(node * BLOCK, BLOCK), BLOCK)

    def place(link):
        safe = jnp.maximum(link, 0)
        lx = lax.div(safe, nz)
        sx = lax.rem(x_me - lx + NX, NX)
        sz = lax.rem(z_me - (safe - lx * nz) + nz, nz)
        return sx * nz + sz, sz * NX + sx

    parent = parents[node]
    link = jnp.where(parent >= 0, lax.div(jnp.maximum(parent, 0), node_count), -1)
    slots, lens = [], [lengths[node]]
    own_slot = jnp.where(node == 0, 0, NX * nz)
    for _ in range(3):
        slot_a, slot_b = place(link)
        slots.append((slot_a, slot_b))
        lens.append(jnp.where(link >= 0, meta_s[slot_a, 1], 0))
        link = jnp.where(link >= 0, meta_s[slot_a, 0], -1)

    cols = 2 * BLOCK
    key_row = lax.broadcasted_iota(jnp.int32, (BLOCK, cols), 0)
    query_col = lax.broadcasted_iota(jnp.int32, (BLOCK, cols), 1)
    query_col = jnp.where(query_col >= BLOCK, query_col - BLOCK, query_col)
    live = lax.broadcasted_iota(jnp.int32, (BLOCK, HEAD), 0) < lens[0]
    masks = [(key_row < lens[0]) & (key_row <= query_col)] + [key_row < m for m in lens[1:]]

    for h in range(2):
        far = far_refs[h]
        acc = acc_refs[h]
        lo, mid, hi = 2 * h * HEAD, (2 * h + 1) * HEAD, (2 * h + 2) * HEAD
        q = jnp.concatenate([q_ref[here, lo:mid], q_ref[here, mid:hi]], axis=0)
        zero = jnp.zeros((), BF16)
        g = jnp.concatenate(
            [jnp.where(live, g_ref[here, lo:mid], zero), jnp.where(live, g_ref[here, mid:hi], zero)], axis=0
        )
        at = slice(h * HEAD, (h + 1) * HEAD)
        keys = [k_ref[here, at]] + [far[s[h], 0:BLOCK, :] for s in slots]
        vals = [v_ref[here, at]] + [far[s[h], BLOCK : 2 * BLOCK, :] for s in slots]
        squash, weight, grad = [], [], []
        total = jnp.zeros((1, cols), F32)
        mixed = jnp.zeros((1, cols), F32)
        for b in range(4):
            t = jnp.tanh(dot(keys[b], q, 1, 1) * (scale / SOFTCAP))
            e = jnp.where(masks[b], jnp.exp(SOFTCAP * t), 0.0)
            d = dot(vals[b], g, 1, 1)
            total += jnp.sum(e, axis=0, keepdims=True)
            mixed += jnp.sum(e * d, axis=0, keepdims=True)
            squash.append(t)
            weight.append(e)
            grad.append(d)
        inverse = 1.0 / total
        delta = mixed * inverse
        query_grad = jnp.zeros((HEAD, cols), F32)
        for b in range(4):
            p = weight[b] * inverse
            ds = (p * (grad[b] - delta) * (scale - scale * (squash[b] * squash[b]))).astype(BF16)
            dk = dot(ds, q, 1, 0)
            dv = dot(p.astype(BF16), g, 1, 0)
            query_grad += dot(keys[b], ds, 0, 0)
            if b == 0:
                kg_ref[here, at] = dk.astype(BF16)
                vg_ref[here, at] = dv.astype(BF16)

            slot = slots[b - 1][h] if b else own_slot
            acc[slot, 0:BLOCK, :] += dk
            acc[slot, BLOCK:, :] += dv
        qg_ref[lo:mid, here] = query_grad[:, :BLOCK].astype(BF16)
        qg_ref[mid:hi, here] = query_grad[:, BLOCK:].astype(BF16)


def main_call(nz, parents, lengths, spot, queries, keys, values, out_grad, query_weight, parts):
    node_count = parents.shape[0]
    rows, cols = queries.shape
    kv_cols = keys.shape[1]
    width = query_weight.shape[0]
    dp = NX * nz
    half = nz // 2
    any_spec = pl.BlockSpec(memory_space=pl.ANY)
    smem = pl.BlockSpec(memory_space=pltpu.SMEM)
    sizes = [nz, nz, nz, half, half] + [NX] * nz
    return pl.pallas_call(
        functools.partial(main_kernel, node_count, nz),
        in_specs=[smem] * 3 + [any_spec] * (10 + nz),
        out_specs=[any_spec] * (8 + nz),
        out_shape=[
            jax.ShapeDtypeStruct((rows, kv_cols), BF16),
            jax.ShapeDtypeStruct((rows, kv_cols), BF16),
            jax.ShapeDtypeStruct((width, rows), BF16),
        ]
        + [jax.ShapeDtypeStruct((size, 2 * BLOCK, HEAD), BF16) for size in sizes],
        scratch_shapes=[
            pltpu.VMEM((rows, cols), BF16),
            pltpu.VMEM((rows, kv_cols), BF16),
            pltpu.VMEM((rows, kv_cols), BF16),
            pltpu.VMEM((rows, cols), BF16),
            pltpu.VMEM((width, cols), BF16),
            pltpu.VMEM((rows, kv_cols), BF16),
            pltpu.VMEM((rows, kv_cols), BF16),
            pltpu.VMEM((cols, rows), BF16),
            pltpu.VMEM((width, rows), BF16),
            pltpu.VMEM((dp, 2 * BLOCK + META, HEAD), BF16),
            pltpu.VMEM((dp, 2 * BLOCK, HEAD), BF16),
            pltpu.VMEM((dp + 1, 2 * BLOCK, HEAD), F32),
            pltpu.VMEM((dp + 1, 2 * BLOCK, HEAD), F32),
            pltpu.VMEM((dp, 2 * BLOCK, HEAD), BF16),
            pltpu.VMEM((dp, 2 * BLOCK, HEAD), BF16),
            pltpu.VMEM((dp, HEAD), jnp.int32),
            pltpu.SMEM((dp, HEAD), jnp.int32),
            pltpu.SemaphoreType.DMA((4,)),
            pltpu.SemaphoreType.DMA((5 + nz,)),
            pltpu.SemaphoreType.DMA((5 + nz,)),
            pltpu.SemaphoreType.DMA((2,)),
            pltpu.SemaphoreType.DMA((TILES,)),
            pltpu.SemaphoreType.DMA((2,)),
        ],
        compiler_params=pltpu.CompilerParams(vmem_limit_bytes=58 * 1024 * 1024),
        name="attention",
    )(parents, lengths, spot, queries, keys, values, out_grad, query_weight, *parts)


def local(queries, keys, values, out_grad, query_weight, parents, lengths, *, dp):
    node_count = parents.shape[0]
    kv_cols = keys.shape[1]
    nz = dp // NX
    half = nz // 2

    def send(array, dx, dz):
        pairs = [
            (x * nz + z, ((x + dx) % NX) * nz + (z + dz) % nz) for x in range(NX) for z in range(nz)
        ]
        return lax.ppermute(array, "dp", pairs)

    def add(*terms):
        return sum(t.astype(F32) for t in terms).astype(BF16)

    me = lax.axis_index("dp")
    spot = jnp.stack([me // nz, me % nz]).astype(jnp.int32)
    smem = pl.BlockSpec(memory_space=pltpu.SMEM)
    pack_a, pack_b = pl.pallas_call(
        functools.partial(pack_kernel, node_count),
        grid=(1,),
        in_specs=[smem, smem] + [pl.BlockSpec((BLOCK, kv_cols), lambda i: (0, 0))] * 2,
        out_specs=[
            pl.BlockSpec((2 * BLOCK + META, HEAD), lambda i: (0, 0)),
            pl.BlockSpec((2 * BLOCK, HEAD), lambda i: (0, 0)),
        ],
        out_shape=[
            jax.ShapeDtypeStruct((2 * BLOCK + META, HEAD), BF16),
            jax.ShapeDtypeStruct((2 * BLOCK, HEAD), BF16),
        ],
        name="pack",
    )(parents, lengths, keys, values)

    a1, a7, a2, a6 = (send(pack_a, 0, s) for s in (1, -1, 2, -2))
    b1, b3 = send(pack_b, 1, 0), send(pack_b, -1, 0)
    b2 = send(b1, 1, 0)
    near_b = jnp.stack([pack_b, b1, b2, b3])
    a34 = send(jnp.stack([a1, a2]), 0, 2)
    a5 = send(a7, 0, -2)
    rings = [near_b] + [None] * (nz - 1)
    for s in range(1, half + 1):
        rings[s] = send(rings[s - 1], 0, 1)
        if s < half:
            rings[nz - s] = send(rings[(nz - s + 1) % nz], 0, -1)
    near_a = jnp.concatenate([jnp.stack([pack_a, a1, a2]), a34, jnp.stack([a5, a6, a7])])
    after, before = send(near_a, 1, 0), send(near_a, -1, 0)
    parts = [near_a, after, before, send(after[:half], 1, 0), send(before[half:], -1, 0)] + rings

    outs = main_call(nz, parents, lengths, spot, queries, keys, values, out_grad, query_weight, parts)
    key_grad, value_grad, hidden = outs[:3]
    own, prev, succ, far_low, far_high = outs[3:8]
    terms = outs[8:]

    hidden_grad = lax.psum_scatter(hidden, "tensor", scatter_dimension=0, tiled=True)

    low_a, high_a = send(far_low, -1, 0), send(far_high, 1, 0)
    low, high = send(terms[half], 0, -1), send(terms[half + 1], 0, 1)
    low_a = send(jnp.concatenate([add(prev[:half], low_a), prev[half:]]), -1, 0)
    high_a = send(jnp.concatenate([succ[:half], add(succ[half:], high_a)]), 1, 0)
    for s in range(half - 1, 0, -1):
        low = send(add(terms[s], low), 0, -1)
    for s in range(half + 2, nz):
        high = send(add(terms[s], high), 0, 1)
    line = [add(own[s], low_a[s], high_a[s]) for s in range(nz)]
    s6 = send(line[6], 0, 2)
    s34 = send(jnp.stack(line[3:5]), 0, -2)
    s5 = send(line[5], 0, 2)
    s1 = send(add(line[1], s34[0]), 0, -1)
    s2 = send(add(line[2], s34[1]), 0, -2)
    s7 = send(add(line[7], s5), 0, 1)
    sum_a = add(line[0], s1, s2, s6, s7)
    line_b = [add(terms[0][s], low[s], high[s]) for s in range(NX)]
    sum_b = add(line_b[0], *[send(line_b[s], -s, 0) for s in range(1, NX)])
    first_key = jnp.concatenate([sum_a[:BLOCK], sum_b[:BLOCK]], axis=1)
    first_value = jnp.concatenate([sum_a[BLOCK:], sum_b[BLOCK:]], axis=1)
    key_grad = lax.dynamic_update_slice(key_grad, first_key, (0, 0))
    value_grad = lax.dynamic_update_slice(value_grad, first_value, (0, 0))
    return (key_grad, value_grad, hidden_grad)


def solution(mesh):
    in_specs = (
        P("dp", "tensor"),
        P("dp", "tensor"),
        P("dp", "tensor"),
        P("dp", "tensor"),
        P(None, "tensor"),
        P("dp"),
        P("dp"),
    )
    out_specs = (P("dp", "tensor"), P("dp", "tensor"), P("tensor", "dp"))
    return jax.shard_map(
        functools.partial(local, dp=mesh.shape["dp"]),
        mesh=mesh,
        in_specs=in_specs,
        out_specs=out_specs,
        check_vma=False,
    )
```
